32 devices in a mesh: groups: 2 (over y), pool: 4 (over z), tensor: 2 (over x), sub: 2 (over core).
Axes of the slice: x: 2, y: 2, z: 4, core: 2. Of those that a mesh axis runs over, the one named last changes fastest.
Arguments:
- patches: bfloat16 [1280, 8192], P(('tensor', 'sub'), ('groups', 'pool')), parts along dimension 1, may hold values from -6 to 6
- window_ids: int32 [32, 256], P(('groups', 'pool')), parts along dimension 0, may hold values from 0 to 5, never falling along the last dimension, each value on 1 to 64 neighbouring positions
- block_route: int32 [32], P('groups'), parts along dimension 0, may hold values from 0 to 3, as said below
- norm_gain: float32 [1280], P(('tensor', 'sub')), may hold values from 0.25 to 1.75
- qkv_weight: bfloat16 [3, 1280, 1280], P(None, None, ('tensor', 'sub')), may hold values from -0.15625 to 0.15625
- qkv_bias: float32 [3, 1280], P(None, ('tensor', 'sub')), may hold values from -3 to 3
- proj_weight: bfloat16 [1280, 1280], P(('tensor', 'sub')), may hold values from -0.15625 to 0.15625
- proj_bias: float32 [1280], P(('tensor', 'sub')), may hold values from -3 to 3
- merge_gain: float32 [1280], P(('tensor', 'sub')), may hold values from 0.25 to 1.75
- w1: bfloat16 [4, 1280, 2560], P(None, ('tensor', 'sub'), 'pool'), may hold values from -0.078125 to 0.078125
- b1: float32 [2560], P(('tensor', 'sub')), may hold values from -3 to 3
- w2: bfloat16 [2560, 8192], P('pool', ('tensor', 'sub')), may hold values from -0.125 to 0.125
- b2: float32 [8192], P(('tensor', 'sub')), may hold values from -2 to 2
- llm_gain: float32 [8192], P(('tensor', 'sub')), may hold values from 0.25 to 1.75
Outputs:
- image_embeds: bfloat16 [8192, 2048], P(('tensor', 'sub'), ('groups', 'pool')), parts along dimension 1
- normed_embeds: bfloat16 [8192, 2048], P(('tensor', 'sub'), ('groups', 'pool')), parts along dimension 1
The draws below stay inside these ranges and needn't reach their ends.
There are 2 independent parts, one for each index of `groups`. The reference program is written for one: setup_inputs(seed, part) draws one part's arguments, and reference() takes and returns one part's arrays. A program takes and returns all parts, laid end to end along the dimension named above; an argument that names none is the same for every part. Nothing has to cross between parts.
Inputs may be any that keep to these rules, and one draw needn't show every extreme that they name: `window_ids`: window ids never fall along a block; each window holds at most 64 patches. `block_route`: at most 2 blocks of one pool group's 4 go to one pool index, and at most 4 blocks of all go to one pool index; both bounds are reached.
All inputs are finite; a program needn't handle non-finite values.
Results may differ from the reference program's by a relative error of at most 0.018.
Values may be sent and summed in bfloat16 or wider, within the bound.
A program may use at most 128 MiB of HBM per device.

```python
import math
import jax
import jax.numpy as jnp
import numpy as np
from jax import lax

VD = 1280
HEADS = 16
HDIM = 80
LD = 8192
MHID = 2560
PB = 256
WIN = 64
SLOTS = 4
HOTK = 1
MAXIN = 4
MROWS = 64
WINC = 6
N_POOL = 4
N_TENSOR = 2
N_SUB = 2


def draw_block_route(key, part):
    key = jax.random.fold_in(key, 7)
    key_dest, key_group, key_slot = jax.random.split(key, 3)
    source = jnp.arange(N_POOL, dtype=jnp.int32)[:, None]
    position = jnp.arange(SLOTS, dtype=jnp.int32)[None, :]
    pattern = jnp.where(position < 2, source // HOTK, (source + position) % N_POOL)
    relabel = jax.random.permutation(key_dest, N_POOL).astype(jnp.int32)
    routed = relabel[pattern]
    routed = routed[jax.random.permutation(key_group, N_POOL)]
    routed = jax.random.permutation(key_slot, routed, axis=1, independent=True)
    return routed.reshape(-1).astype(jnp.int32)


def block_scale(rng, extent, shards, least, largest):
    level, own = 1.0, jax.random.fold_in(rng, 6)
    for dim, shards_of in shards:
        draws = jnp.exp(jax.random.uniform(jax.random.fold_in(own, dim), (shards_of,), jnp.float32, least / len(shards), largest / len(shards)))
        level = level * jnp.repeat(draws, extent[dim] // shards_of).reshape([-1 if axis == dim else 1 for axis in range(len(extent))])
    return level


def split_up(amount, total, limit, lean):
    portions = [(1 << 20) // math.isqrt(grade ** lean) + 1 for grade in range(2, amount + 1)]
    rest, given = total - limit - (amount - 1), [1] * (amount - 1)
    while rest > 0:
        movable = [i for i in range(amount - 1) if given[i] < limit]
        mass, left = sum([portions[i] for i in movable]), rest
        for i in movable:
            extra = min(limit - given[i], max(1, left * portions[i] // mass), rest)
            given[i] = given[i] + extra
            rest = rest - extra
    return np.array([limit] + given)


def ragged_sizes(stream_key, amount, total, reach, lean):
    if amount == 2:
        one = jax.random.randint(stream_key, (), max(1, total - reach), min(reach, total - 1) + 1)
        return jnp.stack([one, total - one])
    lengths = jnp.asarray(split_up(amount, total, reach, lean), jnp.int32)
    pairs = (amount - 1) // 2
    source_of, sink = lengths[1:1 + 2 * pairs:2], lengths[2:2 + 2 * pairs:2]
    room = jnp.minimum(source_of - 1, reach - sink)
    passed = jax.random.randint(jax.random.fold_in(stream_key, 1), (pairs,), 0, 1 << 20) % (room + 1)
    lengths = lengths.at[1:1 + 2 * pairs:2].set(source_of - passed).at[2:2 + 2 * pairs:2].set(sink + passed)
    return lengths[jax.random.permutation(jax.random.fold_in(stream_key, 2), amount)]


def gaussian(stream_key, shape, spread, bound, pieces=(), held_as=jnp.bfloat16):
    array = jax.random.normal(stream_key, shape, jnp.float32) * spread
    if len(pieces) > 0:
        array = block_scale(stream_key, shape, pieces, -0.22, 0.18) * array
    return jnp.clip(array, min=-bound, max=bound).astype(held_as)


def setup_inputs(seed: int = 0, part: int = 0) -> dict:
    key_of = jax.random.split(jax.random.key(seed), 15)
    part_splits = jax.random.split(jax.random.fold_in(key_of[14], part), 15)
    return {
        "patches": gaussian(part_splits[0], (VD, N_POOL * SLOTS * PB), 1.0, 6.0, ((0, 4), (1, 4))),
        "window_ids": jax.vmap(lambda own: jnp.searchsorted(jnp.cumsum(ragged_sizes(own, WINC, PB, WIN, 1)), jnp.arange(PB), side="right"))(jax.random.split(part_splits[1], (N_POOL * SLOTS))).reshape((N_POOL * SLOTS, PB)).astype(jnp.int32),
        "block_route": draw_block_route(jax.random.fold_in(jax.random.fold_in(key_of[14], part), 71), part),
        "norm_gain": jnp.clip(1.0 + 0.15 * jax.random.normal(key_of[3], (VD,), jnp.float32), 0.25, 1.75),
        "qkv_weight": gaussian(key_of[4], (3, VD, VD), VD ** -0.5, 0.15625, ((2, 4),)),
        "qkv_bias": gaussian(key_of[5], (3, VD), 0.5, 3.0, ((1, 4),), jnp.float32),
        "proj_weight": gaussian(key_of[6], (VD, VD), VD ** -0.5, 0.15625, ((0, 4),)),
        "proj_bias": gaussian(key_of[7], (VD,), 0.5, 3.0, ((0, 4),), jnp.float32),
        "merge_gain": jnp.clip(1.0 + 0.15 * jax.random.normal(key_of[8], (VD,), jnp.float32), 0.25, 1.75),
        "w1": gaussian(key_of[9], (4, VD, MHID), (4 * VD) ** -0.5, 0.078125, ((1, 4), (2, 4))),
        "b1": gaussian(key_of[10], (MHID,), 0.5, 3.0, ((0, 4),), jnp.float32),
        "w2": gaussian(key_of[11], (MHID, LD), MHID ** -0.5, 0.125, ((0, 4), (1, 4))),
        "b2": gaussian(key_of[12], (LD,), 0.3, 2.0, ((0, 4),), jnp.float32),
        "llm_gain": jnp.clip(1.0 + 0.15 * jax.random.normal(key_of[13], (LD,), jnp.float32), 0.25, 1.75),
    }


EPSILON = 1e-06

def grouped_sum(terms_fn, operands, shape):

    def add_group(total, pair):
        term = terms_fn(pair).astype(jnp.bfloat16)
        term = lax.optimization_barrier(term)
        return (total + term.astype(jnp.float32), None)
    total, _ = lax.scan(add_group, jnp.zeros(shape, jnp.float32), operands)
    return total

def reference(patches, window_ids, block_route, norm_gain, qkv_weight, qkv_bias, proj_weight, proj_bias, merge_gain, w1, b1, w2, b2, llm_gain):
    groups = N_TENSOR * N_SUB
    feature_share = VD // groups
    blocks_all = N_POOL * SLOTS
    columns = blocks_all * PB
    merged_count = columns // 4
    feats = patches.astype(jnp.float32)
    patch_in = (feats * lax.rsqrt(lax.optimization_barrier(jnp.mean(feats * feats, 0)) + EPSILON)[None, :] * norm_gain[:, None]).astype(jnp.bfloat16)
    qkv = jnp.einsum('cio,in->con', qkv_weight.astype(jnp.float32), patch_in.astype(jnp.float32)) + qkv_bias[:, :, None]
    qkv = qkv.astype(jnp.bfloat16).reshape(3, HEADS, HDIM, blocks_all, PB)
    same_window = window_ids[:, :, None] == window_ids[:, None, :]
    scale = HDIM ** (-0.5)

    def one_head(triple):
        queries, key_rows, value_rows = triple
        scores = jnp.einsum('dbi,dbj->bij', queries.astype(jnp.float32), key_rows.astype(jnp.float32)) * scale
        scores = jnp.where(same_window, scores, -1e+30)
        row_peak = lax.optimization_barrier(jnp.max(scores, -1, keepdims=True))
        exponent = jnp.exp(scores - row_peak)
        attention_weights = (exponent / lax.optimization_barrier(jnp.sum(exponent, -1, keepdims=True))).astype(jnp.bfloat16)
        return jnp.einsum('bij,dbj->dbi', attention_weights.astype(jnp.float32), value_rows.astype(jnp.float32)).astype(jnp.bfloat16)
    context = lax.map(one_head, (qkv[0], qkv[1], qkv[2])).reshape(VD, columns)

    def proj_group(pair):
        part_ctx, part_weight = pair
        return jnp.dot(part_weight.T, part_ctx, preferred_element_type=jnp.float32)
    attn_out = grouped_sum(proj_group, (context.reshape(groups, feature_share, columns), proj_weight.reshape(groups, feature_share, VD)), (VD, columns))
    patch_out = (feats + attn_out + proj_bias[:, None]).astype(jnp.bfloat16)
    out_f = patch_out.astype(jnp.float32)
    merge_in = (out_f * lax.rsqrt(lax.optimization_barrier(jnp.mean(out_f * out_f, 0)) + EPSILON)[None, :] * merge_gain[:, None]).astype(jnp.bfloat16)
    merged = merge_in.reshape(VD, merged_count, 4).transpose(2, 0, 1)

    def hidden_group(pair):
        part_merged, part_weight = pair
        return jnp.einsum('jfc,jfm->cm', part_weight.astype(jnp.float32), part_merged.astype(jnp.float32))
    merged_groups = merged.reshape(4, groups, feature_share, merged_count).transpose(1, 0, 2, 3)
    weight_groups = w1.reshape(4, groups, feature_share, MHID).transpose(1, 0, 2, 3)
    hidden_sum = grouped_sum(hidden_group, (merged_groups, weight_groups), (MHID, merged_count))
    hidden = jax.nn.gelu(hidden_sum + b1[:, None], approximate=False).astype(jnp.bfloat16)
    hidden_blocks = hidden.reshape(MHID, blocks_all, MROWS)
    dest_hot = (block_route[:, None] == jnp.arange(N_POOL, dtype=jnp.int32)[None, :]).astype(jnp.int32)
    earlier = jnp.cumsum(dest_hot, 0) - dest_hot
    block_rank = lax.optimization_barrier(jnp.sum(earlier * dest_hot, 1))
    select = (block_route[None, None, :] == jnp.arange(N_POOL, dtype=jnp.int32)[:, None, None]) & (block_rank[None, None, :] == jnp.arange(MAXIN, dtype=jnp.int32)[None, :, None])
    received = jnp.einsum('qkn,fnr->fqkr', select.astype(jnp.float32), hidden_blocks.astype(jnp.float32))
    received = received.astype(jnp.bfloat16).reshape(MHID, N_POOL * MAXIN * MROWS)
    counts = lax.optimization_barrier(jnp.sum(dest_hot, 0))
    live_mask = (jnp.arange(MAXIN, dtype=jnp.int32)[None, :] < counts[:, None]).astype(jnp.float32)
    live_rows = jnp.broadcast_to(live_mask[:, :, None], (N_POOL, MAXIN, MROWS)).reshape(-1)
    projected = jnp.dot(w2.T, received, preferred_element_type=jnp.float32)
    image_embeds = ((projected + b2[:, None]) * live_rows[None, :]).astype(jnp.bfloat16)
    embed_f = image_embeds.astype(jnp.float32)
    normed_embeds = (embed_f * lax.rsqrt(lax.optimization_barrier(jnp.mean(embed_f * embed_f, 0)) + EPSILON)[None, :] * llm_gain[:, None]).astype(jnp.bfloat16)
    return (image_embeds, normed_embeds)
```

```python
import jax
import jax.numpy as jnp
from jax import lax
from jax.sharding import PartitionSpec as P

HDIM = 80


EPSILON = 1e-06


def shards(
    patches,
    window_ids,
    block_route,
    norm_gain,
    qkv_weight,
    qkv_bias,
    proj_weight,
    proj_bias,
    merge_gain,
    w1,
    b1,
    w2,
    b2,
    llm_gain,
):
    feature_share, local_cols = patches.shape
    vision_width = qkv_weight.shape[1]
    groups = lax.axis_size(("tensor", "sub"))
    pool_count = lax.axis_size("pool")
    my_pool = lax.axis_index("pool")
    block_slots, block_len = window_ids.shape
    merged_rows = block_len // 4
    feats = patches.astype(jnp.float32)
    squares = lax.psum(jnp.sum(feats * feats, 0), ("tensor", "sub"))
    patch_in = (
        feats * lax.rsqrt(squares / vision_width + EPSILON)[None, :] * norm_gain[:, None]
    ).astype(jnp.bfloat16)
    weight_rows = qkv_weight
    qkv_total = jnp.einsum(
        "cio,in->con",
        weight_rows,
        lax.all_gather(patch_in, ("tensor", "sub"), axis=0, tiled=True),
        preferred_element_type=jnp.float32,
    )
    qkv = (qkv_total + qkv_bias[:, :, None]).astype(jnp.bfloat16)
    head_count = feature_share // HDIM
    qkv = qkv.reshape(3, head_count, HDIM, block_slots, block_len)
    same_window = window_ids[:, :, None] == window_ids[:, None, :]
    scores = jnp.einsum(
        "hdbi,hdbj->hbij", qkv[0], qkv[1], preferred_element_type=jnp.float32
    ) * HDIM ** (-0.5)
    scores = jnp.where(same_window[None], scores, -1e30)
    row_peak = jnp.max(scores, -1, keepdims=True)
    exponent = jnp.exp(scores - row_peak)
    attention_weights = (exponent / jnp.sum(exponent, -1, keepdims=True)).astype(jnp.bfloat16)
    context = jnp.einsum(
        "hbij,hdbj->hdbi", attention_weights, qkv[2], preferred_element_type=jnp.float32
    )
    context = context.astype(jnp.bfloat16).reshape(feature_share, local_cols)
    attn_out = lax.psum_scatter(
        jnp.einsum("hc,hn->cn", proj_weight, context, preferred_element_type=jnp.float32).astype(
            jnp.bfloat16
        ),
        ("tensor", "sub"),
        scatter_dimension=0,
        tiled=True,
    ).astype(jnp.float32)
    patch_out = (feats + attn_out + proj_bias[:, None]).astype(jnp.bfloat16)
    out_f = patch_out.astype(jnp.float32)
    merge_squares = lax.psum(jnp.sum(out_f * out_f, 0), ("tensor", "sub"))
    merge_in = (
        out_f * lax.rsqrt(merge_squares / vision_width + EPSILON)[None, :] * merge_gain[:, None]
    ).astype(jnp.bfloat16)
    merged = merge_in.reshape(feature_share, local_cols // 4, 4).transpose(2, 0, 1)
    merged_all = lax.all_gather(merged, "pool", axis=2, tiled=True)
    hidden_share = w1.shape[2]
    hidden_full = lax.psum(
        jnp.einsum("jfc,jfm->cm", w1, merged_all, preferred_element_type=jnp.float32).astype(
            jnp.bfloat16
        ),
        ("tensor", "sub"),
    ).astype(jnp.float32)
    bias_all = lax.all_gather(b1, ("tensor", "sub"), axis=0, tiled=True)
    bias_mine = lax.dynamic_slice_in_dim(bias_all, my_pool * hidden_share, hidden_share, 0)
    hidden = jax.nn.gelu(hidden_full + bias_mine[:, None], approximate=False).astype(jnp.bfloat16)
    block_total = block_route.shape[0]
    hidden_blocks = hidden.reshape(hidden_share, block_total, merged_rows)
    hot_groups = max(1, pool_count // 16)
    capacity_in = 2 * hot_groups + block_slots - 2
    pool_index = jnp.arange(pool_count, dtype=jnp.int32)
    goes = (block_route[None, :] == pool_index[:, None]).astype(jnp.int32)
    rank = jnp.cumsum(goes, 1) - goes
    slot_index = jnp.arange(capacity_in, dtype=jnp.int32)
    select = (
        (goes[:, None, :] == 1) & (rank[:, None, :] == slot_index[None, :, None])
    ).astype(jnp.bfloat16)
    routed = jnp.einsum(
        "qkn,fnr->fqkr", select, hidden_blocks, preferred_element_type=jnp.float32
    ).astype(jnp.bfloat16)
    routed = routed.reshape(hidden_share, pool_count, capacity_in * merged_rows)
    partial = jnp.einsum("hc,hqn->qcn", w2, routed, preferred_element_type=jnp.float32)
    projected = lax.psum_scatter(
        partial.astype(jnp.bfloat16), "pool", scatter_dimension=0, tiled=True
    )[0].astype(jnp.float32)
    count_mine = jnp.sum((block_route == my_pool).astype(jnp.int32))
    live_mask = (slot_index < count_mine).astype(jnp.float32)
    live_rows = jnp.broadcast_to(live_mask[:, None], (capacity_in, merged_rows)).reshape(-1)
    image_embeds = ((projected + b2[:, None]) * live_rows[None, :]).astype(jnp.bfloat16)
    embed_f = image_embeds.astype(jnp.float32)
    embed_squares = lax.psum(jnp.sum(embed_f * embed_f, 0), ("tensor", "sub"))
    normed_embeds = (
        embed_f
        * lax.rsqrt(embed_squares / (w2.shape[1] * groups) + EPSILON)[None, :]
        * llm_gain[:, None]
    ).astype(jnp.bfloat16)
    return (image_embeds, normed_embeds)


def solution(mesh):
    placed = (
        P(("tensor", "sub"), ("groups", "pool")),
        P(("groups", "pool"), None),
        P("groups"),
        P(("tensor", "sub")),
        P(None, None, ("tensor", "sub")),
        P(None, ("tensor", "sub")),
        P(("tensor", "sub"), None),
        P(("tensor", "sub")),
        P(("tensor", "sub")),
        P(None, ("tensor", "sub"), "pool"),
        P(("tensor", "sub")),
        P("pool", ("tensor", "sub")),
        P(("tensor", "sub")),
        P(("tensor", "sub")),
    )
    return jax.shard_map(
        shards,
        mesh=mesh,
        in_specs=placed,
        out_specs=(
            P(("tensor", "sub"), ("groups", "pool")),
            P(("tensor", "sub"), ("groups", "pool")),
        ),
        check_vma=False,
    )
```

```python
import functools

import jax
import jax.numpy as jnp
from jax import lax
from jax.experimental import pallas as pl
from jax.experimental.pallas import tpu as pltpu
from jax.sharding import PartitionSpec as P

HDIM = 80


EPSILON = 1e-06


def shards(
    patches,
    window_ids,
    block_route,
    norm_gain,
    qkv_weight,
    qkv_bias,
    proj_weight,
    proj_bias,
    merge_gain,
    w1,
    b1,
    w2,
    b2,
    llm_gain,
):
    feature_share, local_cols = patches.shape
    vision_width = qkv_weight.shape[1]
    groups = lax.axis_size(("tensor", "sub"))
    pool_count = lax.axis_size("pool")
    my_pool = lax.axis_index("pool")
    block_slots, block_len = window_ids.shape
    merged_rows = block_len // 4
    feats = patches.astype(jnp.float32)
    squares = lax.psum(jnp.sum(feats * feats, 0), ("tensor", "sub"))
    patch_in = (
        feats * lax.rsqrt(squares / vision_width + EPSILON)[None, :] * norm_gain[:, None]
    ).astype(jnp.bfloat16)
    weight_rows = qkv_weight
    qkv_total = jnp.einsum(
        "cio,in->con",
        weight_rows,
        lax.all_gather(patch_in, ("tensor", "sub"), axis=0, tiled=True),
        preferred_element_type=jnp.float32,
    )
    qkv = (qkv_total + qkv_bias[:, :, None]).astype(jnp.bfloat16)
    head_count = feature_share // HDIM
    qkv = qkv.reshape(3, head_count, HDIM, block_slots, block_len)
    same_window = window_ids[:, :, None] == window_ids[:, None, :]
    scores = jnp.einsum(
        "hdbi,hdbj->hbij", qkv[0], qkv[1], preferred_element_type=jnp.float32
    ) * HDIM ** (-0.5)
    scores = jnp.where(same_window[None], scores, -1e30)
    row_peak = jnp.max(scores, -1, keepdims=True)
    exponent = jnp.exp(scores - row_peak)
    attention_weights = (exponent / jnp.sum(exponent, -1, keepdims=True)).astype(jnp.bfloat16)
    context = jnp.einsum(
        "hbij,hdbj->hdbi", attention_weights, qkv[2], preferred_element_type=jnp.float32
    )
    context = context.astype(jnp.bfloat16).reshape(feature_share, local_cols)
    attn_out = lax.psum_scatter(
        jnp.einsum("hc,hn->cn", proj_weight, context, preferred_element_type=jnp.float32).astype(
            jnp.bfloat16
        ),
        ("tensor", "sub"),
        scatter_dimension=0,
        tiled=True,
    ).astype(jnp.float32)
    patch_out = (feats + attn_out + proj_bias[:, None]).astype(jnp.bfloat16)
    out_f = patch_out.astype(jnp.float32)
    merge_squares = lax.psum(jnp.sum(out_f * out_f, 0), ("tensor", "sub"))
    merge_in = (
        out_f * lax.rsqrt(merge_squares / vision_width + EPSILON)[None, :] * merge_gain[:, None]
    ).astype(jnp.bfloat16)
    merged = merge_in.reshape(feature_share, local_cols // 4, 4).transpose(2, 0, 1)
    merged_all = lax.all_gather(merged, "pool", axis=2, tiled=True)
    hidden_share = w1.shape[2]
    hidden_full = lax.psum(
        jnp.einsum("jfc,jfm->cm", w1, merged_all, preferred_element_type=jnp.float32).astype(
            jnp.bfloat16
        ),
        ("tensor", "sub"),
    ).astype(jnp.float32)
    bias_all = lax.all_gather(b1, ("tensor", "sub"), axis=0, tiled=True)
    bias_mine = lax.dynamic_slice_in_dim(bias_all, my_pool * hidden_share, hidden_share, 0)
    hidden = jax.nn.gelu(hidden_full + bias_mine[:, None], approximate=False).astype(jnp.bfloat16)
    block_total = block_route.shape[0]
    hidden_blocks = hidden.reshape(hidden_share, block_total, merged_rows)
    hot_groups = max(1, pool_count // 16)
    capacity_in = 2 * hot_groups + block_slots - 2
    pool_index = jnp.arange(pool_count, dtype=jnp.int32)
    goes = (block_route[None, :] == pool_index[:, None]).astype(jnp.int32)
    rank = jnp.cumsum(goes, 1) - goes
    slot_index = jnp.arange(capacity_in, dtype=jnp.int32)
    select = (
        (goes[:, None, :] == 1) & (rank[:, None, :] == slot_index[None, :, None])
    ).astype(jnp.bfloat16)
    routed = jnp.einsum(
        "qkn,fnr->fqkr", select, hidden_blocks, preferred_element_type=jnp.float32
    ).astype(jnp.bfloat16)
    routed = routed.reshape(hidden_share, pool_count, capacity_in * merged_rows)
    partial = jnp.einsum("hc,hqn->qcn", w2, routed, preferred_element_type=jnp.float32)
    projected = lax.psum_scatter(
        partial.astype(jnp.bfloat16), "pool", scatter_dimension=0, tiled=True
    )[0].astype(jnp.float32)
    count_mine = jnp.sum((block_route == my_pool).astype(jnp.int32))
    live_mask = (slot_index < count_mine).astype(jnp.float32)
    live_rows = jnp.broadcast_to(live_mask[:, None], (capacity_in, merged_rows)).reshape(-1)
    image_embeds = ((projected + b2[:, None]) * live_rows[None, :]).astype(jnp.bfloat16)
    embed_f = image_embeds.astype(jnp.float32)
    embed_squares = lax.psum(jnp.sum(embed_f * embed_f, 0), ("tensor", "sub"))
    normed_embeds = (
        embed_f
        * lax.rsqrt(embed_squares / (w2.shape[1] * groups) + EPSILON)[None, :]
        * llm_gain[:, None]
    ).astype(jnp.bfloat16)
    return (image_embeds, normed_embeds)


def fused_kernel(
    vision_width, model_width, patches, ids_row, tall, fcols, small, qkv_w, pw, w1, w2, lcols, live,
    img, nrm,
    xall, sall, pwall, gcol, xin, qkv, ctxall, zall, pbuf, rsib, csum, rx, hid, rt, obuf, rup, rdn,
    sq, sq2, acc_ref,
    x_send, x_recv, c_send, c_recv, s_send, s_recv, w_send, w_recv, q_send, q_recv,
    z_send, z_recv, h1_send, h1_recv, h2_send, h2_recv, h3_send, h3_recv,
    o_send, u_recv, d_recv, l_send, l_recv,
):
    f32, bf16 = jnp.float32, jnp.bfloat16
    feat, cols = patches.shape
    half_cols = cols // 2
    blocks, block_len = ids_row.shape
    heads = feat // HDIM
    share = w1.shape[2]
    hs = share // 2
    p, tx, sc = lax.axis_index("pool"), lax.axis_index("tensor"), lax.axis_index("sub")
    me, xt, st, dt = tx * 2 + sc, (1 - tx) * 2 + sc, tx * 2 + 1 - sc, (1 - tx) * 2 + 1 - sc
    xp, sib, diag = {"tensor": 1 - tx}, {"sub": 1 - sc}, {"tensor": 1 - tx, "sub": 1 - sc}
    top = zall.shape[0] - 1

    def rcopy(src, dst, ss, rs, dev):
        return pltpu.make_async_remote_copy(
            src_ref=src, dst_ref=dst, send_sem=ss, recv_sem=rs, device_id=dev,
            device_id_type=pl.DeviceIdType.MESH,
        )

    barrier = pltpu.get_barrier_semaphore()
    for dev in (xp, sib, diag):
        pl.semaphore_signal(barrier, inc=1, device_id=dev, device_id_type=pl.DeviceIdType.MESH)

    @pl.when(p > 0)
    def _():
        pl.semaphore_signal(
            barrier, inc=1, device_id={"pool": p - 1}, device_id_type=pl.DeviceIdType.MESH
        )

    @pl.when(p < top)
    def _():
        pl.semaphore_signal(
            barrier, inc=1, device_id={"pool": p + 1}, device_id_type=pl.DeviceIdType.MESH
        )

    for pair in range(2):
        xall[pair, me] = patches[:, pair * half_cols : (pair + 1) * half_cols]
    sall[me] = small[...]
    pwall[me] = pw[me]
    pl.semaphore_wait(barrier, 3 + (p + top - 1) // top + (2 * top - p - 1) // top)

    def gather_start(buf, pair, ssem, rsem):
        own = buf.at[pair, me]
        rcopy(own, own, ssem.at[pair, 0], rsem.at[pair, me], xp).start()
        rcopy(own, own, ssem.at[pair, 1], rsem.at[pair, me], sib).start()

    def gather_finish(buf, pair, ssem, rsem):
        other = buf.at[pair, xt]
        fwd = rcopy(other, other, ssem.at[pair, 2], rsem.at[pair, xt], sib)
        fwd.wait_recv()
        fwd.start()
        for slot in (st, dt):
            rcopy(other, buf.at[pair, slot], ssem.at[pair, 2], rsem.at[pair, slot], sib).wait_recv()

    def gather_drain(buf, pair, ssem, rsem):
        for k in range(3):
            rcopy(buf.at[pair, me], buf.at[pair, me], ssem.at[pair, k], rsem.at[pair, me], sib).wait_send()

    peers = ((xp, xt), (sib, st), (diag, dt))
    for k, (dev, _t) in enumerate(peers):
        rcopy(sall.at[me], sall.at[me], s_send.at[k], s_recv.at[me], dev).start()
    gather_start(xall, 0, x_send, x_recv)
    gather_start(xall, 1, x_send, x_recv)
    for k, (dev, t) in enumerate(peers):
        rcopy(pw.at[t], pwall.at[me], w_send.at[k], w_recv.at[me], dev).start()
    for k, (dev, t) in enumerate(peers):
        rcopy(sall.at[t], sall.at[t], s_send.at[k], s_recv.at[t], dev).wait_recv()

    rows = lax.broadcasted_iota(jnp.int32, (feat, feat), 0)
    lanes = lax.broadcasted_iota(jnp.int32, (feat, feat), 1)
    for t in range(4):
        gcol[t] = jnp.sum(jnp.where(rows == lanes, sall[t, 0:1, :feat], 0.0), 1, keepdims=True)

    def dot0(a, b):
        return lax.dot_general(a, b, (((0,), (0,)), ((), ())), preferred_element_type=f32)

    per_pair = blocks // 2
    for pair in range(2):
        gather_finish(xall, pair, x_send, x_recv)
        total = jnp.zeros((1, half_cols), f32)
        for t in range(4):
            v = xall[pair, t].astype(f32)
            total += jnp.sum(v * v, 0, keepdims=True)
        inv = lax.rsqrt(total / vision_width + EPSILON)
        for t in range(4):
            xin[t * feat : (t + 1) * feat] = (
                xall[pair, t].astype(f32) * inv * gcol[t]
            ).astype(bf16)
        for c in range(3):
            qkv[c] = (dot0(qkv_w[c], xin[...]) + fcols[:, c : c + 1]).astype(bf16)
        for bb in range(per_pair):
            b = pair * per_pair + bb
            lo = bb * block_len
            same = tall[b * block_len : (b + 1) * block_len, 0:1] == ids_row[b : b + 1, :]

            def head(h, carry):
                r = pl.ds(pl.multiple_of(h * HDIM, HDIM), HDIM)
                q = qkv[0, r, lo : lo + block_len]
                k = qkv[1, r, lo : lo + block_len]
                v = qkv[2, r, lo : lo + block_len]
                scores = jnp.where(same, dot0(k, q) * HDIM ** (-0.5), -1e30)
                e = jnp.exp(scores - jnp.max(scores, 0, keepdims=True))
                a = (e / jnp.sum(e, 0, keepdims=True)).astype(bf16)
                ctxall[pair, me, r, lo : lo + block_len] = jnp.dot(
                    v, a, preferred_element_type=f32
                ).astype(bf16)
                return carry

            lax.fori_loop(0, heads, head, 0)
        gather_start(ctxall, pair, c_send, c_recv)

    for k, (dev, t) in enumerate(peers):
        rcopy(pw.at[t], pwall.at[t], w_send.at[k], w_recv.at[t], dev).wait_recv()

    for pair in range(2):
        gather_finish(ctxall, pair, c_send, c_recv)
        total = patches[:, pair * half_cols : (pair + 1) * half_cols].astype(f32) + fcols[:, 3:4]
        for t in range(4):
            total += (
                jnp.dot(pwall[t], ctxall[pair, t], preferred_element_type=f32)
                .astype(bf16)
                .astype(f32)
            )
        out = total.astype(bf16).astype(f32)
        sq[pair, me] = jnp.broadcast_to(jnp.sum(out * out, 0, keepdims=True), (8, half_cols))
        for k, (dev, t) in enumerate(peers):
            rcopy(sq.at[pair, me], sq.at[pair, me], q_send.at[pair, k], q_recv.at[pair, me], dev).start()
        for k, (dev, t) in enumerate(peers):
            rcopy(sq.at[pair, t], sq.at[pair, t], q_send.at[pair, k], q_recv.at[pair, t], dev).wait_recv()
        squares = sq[pair, 0, 0:1] + sq[pair, 1, 0:1] + sq[pair, 2, 0:1] + sq[pair, 3, 0:1]
        merge_in = (
            out * lax.rsqrt(squares / vision_width + EPSILON) * fcols[:, 4:5]
        ).astype(bf16)
        n_i = lax.broadcasted_iota(jnp.int32, (half_cols, half_cols // 4), 0)
        m_i = lax.broadcasted_iota(jnp.int32, (half_cols, half_cols // 4), 1)
        for j in range(4):
            pick = jnp.where(n_i == 4 * m_i + j, 1.0, 0.0).astype(bf16)
            zall[p, pair, j] = jnp.dot(merge_in, pick, preferred_element_type=f32).astype(bf16)
        own = zall.at[p, pair]

        @pl.when(p < top)
        def _():
            rcopy(own, own, z_send.at[0, p, pair], z_recv.at[p, pair], {"pool": p + 1}).start()

        @pl.when(p > 0)
        def _():
            rcopy(own, own, z_send.at[1, p, pair], z_recv.at[p, pair], {"pool": p - 1}).start()

    rows_h = lax.broadcasted_iota(jnp.int32, (hs, hs), 0)
    lanes_h = lax.broadcasted_iota(jnp.int32, (hs, hs), 1)
    base = small.shape[1] - share
    b1_lo = sall[p, 0:1, base : base + hs]
    b1_hi = sall[p, 0:1, base + hs : base + share]
    b1_row = jnp.where(sc == 0, b1_lo, b1_hi)
    b1_col = jnp.sum(jnp.where(rows_h == lanes_h, b1_row, 0.0), 1, keepdims=True)
    acc_ref[:hs, 0:1] = b1_col

    places = 2 * top + 1
    width = half_cols // 4

    def place(k):
        pair, kk = k // places, k % places
        step = (kk + 1) // 2
        return pair, p + step * (1 - 2 * (kk % 2))

    def on_chunk(k, fn):
        pair, src = place(k)

        @pl.when((k >= 0) & (k < 2 * places) & (src >= 0) & (src <= top))
        def _():
            fn(pair, src)

    def step1(pair, src):
        chunk = zall.at[src, pair]

        @pl.when(src != p)
        def _():
            rcopy(chunk, chunk, z_send.at[0, src, pair], z_recv.at[src, pair], sib).wait_recv()

        @pl.when((src < p) & (p < top))
        def _():
            rcopy(chunk, chunk, z_send.at[0, src, pair], z_recv.at[src, pair], {"pool": p + 1}).start()

        @pl.when((src > p) & (p > 0))
        def _():
            rcopy(chunk, chunk, z_send.at[1, src, pair], z_recv.at[src, pair], {"pool": p - 1}).start()

        c = src * 2 + pair
        total = dot0(w1[0], zall[src, pair, 0])
        for j in range(1, 4):
            total += dot0(w1[j], zall[src, pair, j])
        pbuf[c, 0] = total[:hs].astype(bf16)
        pbuf[c, 1] = total[hs:].astype(bf16)
        rcopy(pbuf.at[c, 1 - sc], rsib.at[c], h1_send.at[c], h1_recv.at[c], sib).start()

    def step2(pair, src):
        c = src * 2 + pair
        rcopy(pbuf.at[c, 1 - sc], rsib.at[c], h1_send.at[c], h1_recv.at[c], sib).wait()
        csum[c] = (pbuf[c, sc].astype(f32) + rsib[c].astype(f32)).astype(bf16)
        rcopy(csum.at[c], rx.at[c], h2_send.at[c], h2_recv.at[c], xp).start()

    def hid_copy(c):
        dst = hid.at[sc, :, pl.ds(pl.multiple_of(c * width, width), width)]
        return rcopy(dst, dst, h3_send.at[c], h3_recv.at[c], sib)

    def step3(pair, src):
        c = src * 2 + pair
        rcopy(csum.at[c], rx.at[c], h2_send.at[c], h2_recv.at[c], xp).wait()
        pre = csum[c].astype(f32) + rx[c].astype(f32) + acc_ref[:hs, 0:1]
        act = 0.5 * pre * (1.0 + lax.erf(pre * (0.5**0.5)))
        hid[sc, :, pl.ds(pl.multiple_of(c * width, width), width)] = act.astype(bf16)
        hid_copy(c).start()

    def hidden_step(k, carry):
        on_chunk(k, step1)
        on_chunk(k - 1, step2)
        on_chunk(k - 2, step3)
        return carry

    lax.fori_loop(0, 2 * places + 2, hidden_step, 0)

    def hid_wait(c, carry):
        hid_copy(c).wait_send()
        other = hid.at[1 - sc, :, pl.ds(pl.multiple_of(c * width, width), width)]
        rcopy(other, other, h3_send.at[c], h3_recv.at[c], sib).wait_recv()
        return carry

    lax.fori_loop(0, 2 * (top + 1), hid_wait, 0)

    all_rows = hid.shape[2]
    out_cols = img.shape[1]
    col_i = lax.broadcasted_iota(jnp.int32, (all_rows, out_cols), 1)

    def route(q, carry):
        pick = jnp.where(tall[:all_rows, 1:2] == col_i + q * out_cols, 1.0, 0.0).astype(bf16)
        for half in range(2):
            rt[q, half * hs : (half + 1) * hs] = jnp.dot(
                hid[half], pick, preferred_element_type=f32
            ).astype(bf16)
        return carry

    lax.fori_loop(0, top + 1, route, 0)

    pieces, piece = obuf.shape[1], obuf.shape[2]

    def part(q, r):
        return dot0(w2[:, pl.ds(pl.multiple_of(r * piece, piece), piece)], rt[q])

    def send_one(q, r, buf, sem, dev, has_more, from_dev):
        acc_ref[...] = part(q, r)

        @pl.when(has_more)
        def _():
            rcopy(obuf.at[q, r], buf.at[q, r], o_send.at[q, r], sem.at[q, r], from_dev).wait_recv()
            acc_ref[...] += buf[q, r].astype(f32)

        obuf[q, r] = acc_ref[...].astype(bf16)
        rcopy(obuf.at[q, r], buf.at[q, r], o_send.at[q, r], sem.at[q, r], dev).start()

    def out_step(k, carry):
        delta, r = top - k // pieces, k % pieces

        @pl.when(p + delta <= top)
        def _():
            send_one(p + delta, r, rup, u_recv, {"pool": p + 1}, p > 0, sib)

        @pl.when(p - delta >= 0)
        def _():
            send_one(p - delta, r, rdn, d_recv, {"pool": p - 1}, p < top, sib)

        return carry

    lax.fori_loop(0, top * pieces, out_step, 0)

    def last_step(r, squares):
        rr = pl.ds(pl.multiple_of(r * piece, piece), piece)
        acc_ref[...] = part(p, r) + lcols[rr, 0:1]

        @pl.when(p > 0)
        def _():
            rcopy(obuf.at[p, r], rup.at[p, r], o_send.at[p, r], u_recv.at[p, r], sib).wait_recv()
            acc_ref[...] += rup[p, r].astype(f32)

        @pl.when(p < top)
        def _():
            rcopy(obuf.at[p, r], rdn.at[p, r], o_send.at[p, r], d_recv.at[p, r], sib).wait_recv()
            acc_ref[...] += rdn[p, r].astype(f32)

        res = (acc_ref[...] * live[...]).astype(bf16)
        img[rr, :] = res
        res = res.astype(f32)
        return squares + jnp.sum(res * res, 0, keepdims=True)

    squares = lax.fori_loop(0, pieces, last_step, jnp.zeros((1, out_cols), f32))
    sq2[me] = jnp.broadcast_to(squares, (8, out_cols))
    for k, (dev, t) in enumerate(peers):
        rcopy(sq2.at[me], sq2.at[me], l_send.at[k], l_recv.at[me], dev).start()

    for pair in range(2):
        gather_drain(xall, pair, x_send, x_recv)
        gather_drain(ctxall, pair, c_send, c_recv)
        for k in range(3):
            rcopy(sq.at[pair, me], sq.at[pair, me], q_send.at[pair, k], q_recv.at[pair, me], sib).wait_send()
        for src in range(top + 1):
            chunk = zall.at[src, pair]

            @pl.when((src <= p) & (p < top))
            def _():
                rcopy(chunk, chunk, z_send.at[0, src, pair], z_recv.at[src, pair], sib).wait_send()

            @pl.when((src >= p) & (p > 0))
            def _():
                rcopy(chunk, chunk, z_send.at[1, src, pair], z_recv.at[src, pair], sib).wait_send()

    for k in range(3):
        rcopy(sall.at[me], sall.at[me], s_send.at[k], s_recv.at[me], sib).wait_send()
        rcopy(pw.at[me], pwall.at[me], w_send.at[k], w_recv.at[me], sib).wait_send()
    for q in range(top + 1):

        @pl.when(q != p)
        def _():
            for r in range(pieces):
                rcopy(obuf.at[q, r], rup.at[q, r], o_send.at[q, r], u_recv.at[q, r], sib).wait_send()

    for k, (dev, t) in enumerate(peers):
        rcopy(sq2.at[t], sq2.at[t], l_send.at[k], l_recv.at[t], dev).wait()
    squares = sq2[0, 0:1] + sq2[1, 0:1] + sq2[2, 0:1] + sq2[3, 0:1]
    inv = lax.rsqrt(squares / model_width + EPSILON)

    def norm_step(r, carry):
        rr = pl.ds(pl.multiple_of(r * piece, piece), piece)
        nrm[rr, :] = (img[rr, :].astype(f32) * inv * lcols[rr, 1:2]).astype(bf16)
        return carry

    lax.fori_loop(0, pieces, norm_step, 0)


def fused_shards(
    patches, window_ids, block_route, norm_gain, qkv_weight, qkv_bias, proj_weight, proj_bias,
    merge_gain, w1, b1, w2, b2, llm_gain,
):
    f32, bf16 = jnp.float32, jnp.bfloat16
    feat, cols = patches.shape
    pool = lax.axis_size("pool")
    my_pool = lax.axis_index("pool")
    slots, block_len = window_ids.shape
    width = qkv_weight.shape[1]
    merged_rows = block_len // 4
    hot_groups = max(1, pool // 16)
    capacity = 2 * hot_groups + slots - 2
    out_cols = capacity * merged_rows
    goes = (block_route[:, None] == block_route[None, :]).astype(jnp.int32)
    total = block_route.shape[0]
    index = jnp.arange(total, dtype=jnp.int32)
    rank = jnp.sum(jnp.where(index[None, :] < index[:, None], goes, 0), 1)
    first = jnp.where(rank < capacity, block_route * out_cols + rank * merged_rows, -(1 << 20))
    dest = (first[:, None] + jnp.arange(merged_rows, dtype=jnp.int32)[None, :]).reshape(-1)
    tall = jnp.stack([window_ids.reshape(-1), dest], 1)
    count = jnp.sum((block_route == my_pool).astype(jnp.int32))
    live = (jnp.arange(out_cols, dtype=jnp.int32) // merged_rows < count).astype(f32)[None, :]
    fcols = jnp.concatenate([qkv_bias.T, proj_bias[:, None], merge_gain[:, None]], 1)
    share = w1.shape[2]
    pad = -feat % 128
    row = jnp.concatenate([norm_gain, jnp.zeros((pad,), f32), b1])
    small = jnp.broadcast_to(row[None, :], (8, row.shape[0]))
    pw = proj_weight.reshape(feat, 4, feat).transpose(1, 2, 0)
    lcols = jnp.stack([b2, llm_gain], 1)
    local_out = w2.shape[1]
    hc, hs, wd = cols // 2, share // 2, cols // 8
    n2 = 2 * pool
    pieces = 4
    piece = local_out // pieces
    V, D = pltpu.VMEM, pltpu.SemaphoreType.DMA
    scratch = [
        V((2, 4, feat, hc), bf16), V((4, 8, row.shape[0]), f32), V((4, feat, feat), bf16),
        V((4, feat, 1), f32), V((width, hc), bf16), V((3, feat, hc), bf16),
        V((2, 4, feat, hc), bf16), V((pool, 2, 4, feat, wd), bf16), V((n2, 2, hs, wd), bf16),
        V((n2, hs, wd), bf16), V((n2, hs, wd), bf16), V((n2, hs, wd), bf16),
        V((2, hs, n2 * wd), bf16), V((pool, share, out_cols), bf16),
        V((pool, pieces, piece, out_cols), bf16), V((pool, pieces, piece, out_cols), bf16),
        V((pool, pieces, piece, out_cols), bf16),
        V((2, 4, 8, hc), f32), V((4, 8, out_cols), f32), V((piece, out_cols), f32),
        D((2, 3)), D((2, 4)), D((2, 3)), D((2, 4)), D((3,)), D((4,)), D((3,)), D((4,)),
        D((2, 3)), D((2, 4)), D((2, pool, 2)), D((pool, 2)),
        D((n2,)), D((n2,)), D((n2,)), D((n2,)), D((n2,)), D((n2,)),
        D((pool, pieces)), D((pool, pieces)), D((pool, pieces)), D((3,)), D((4,)),
    ]
    shape = jax.ShapeDtypeStruct((local_out, out_cols), bf16)
    vm = pl.BlockSpec(memory_space=pltpu.VMEM)
    return pl.pallas_call(
        functools.partial(fused_kernel, width, local_out * 4),
        out_shape=(shape, shape),
        in_specs=[vm] * 11,
        out_specs=(vm, vm),
        scratch_shapes=scratch,
        compiler_params=pltpu.CompilerParams(
            collective_id=0, has_side_effects=True, vmem_limit_bytes=60 << 20
        ),
        name="vision_fused",
    )(patches, window_ids, tall, fcols, small, qkv_weight, pw, w1, w2, lcols, live)


def fused_fits(mesh):
    return mesh.shape["tensor"] == 2 and mesh.shape["sub"] == 2 and mesh.shape["pool"] == 4


def solution(mesh):
    placed = (
        P(("tensor", "sub"), ("groups", "pool")),
        P(("groups", "pool"), None),
        P("groups"),
        P(("tensor", "sub")),
        P(None, None, ("tensor", "sub")),
        P(None, ("tensor", "sub")),
        P(("tensor", "sub"), None),
        P(("tensor", "sub")),
        P(("tensor", "sub")),
        P(None, ("tensor", "sub"), "pool"),
        P(("tensor", "sub")),
        P("pool", ("tensor", "sub")),
        P(("tensor", "sub")),
        P(("tensor", "sub")),
    )
    return jax.shard_map(
        fused_shards if fused_fits(mesh) else shards,
        mesh=mesh,
        in_specs=placed,
        out_specs=(
            P(("tensor", "sub"), ("groups", "pool")),
            P(("tensor", "sub"), ("groups", "pool")),
        ),
        check_vma=False,
    )
```

```python
import functools

import jax
import jax.numpy as jnp
from jax import lax
from jax.experimental import pallas as pl
from jax.experimental.pallas import tpu as pltpu
from jax.sharding import PartitionSpec as P

HDIM = 80


EPSILON = 1e-06


def shards(
    patches,
    window_ids,
    block_route,
    norm_gain,
    qkv_weight,
    qkv_bias,
    proj_weight,
    proj_bias,
    merge_gain,
    w1,
    b1,
    w2,
    b2,
    llm_gain,
):
    feature_share, local_cols = patches.shape
    vision_width = qkv_weight.shape[1]
    groups = lax.axis_size(("tensor", "sub"))
    pool_count = lax.axis_size("pool")
    my_pool = lax.axis_index("pool")
    block_slots, block_len = window_ids.shape
    merged_rows = block_len // 4
    feats = patches.astype(jnp.float32)
    squares = lax.psum(jnp.sum(feats * feats, 0), ("tensor", "sub"))
    patch_in = (
        feats * lax.rsqrt(squares / vision_width + EPSILON)[None, :] * norm_gain[:, None]
    ).astype(jnp.bfloat16)
    weight_rows = qkv_weight
    qkv_total = jnp.einsum(
        "cio,in->con",
        weight_rows,
        lax.all_gather(patch_in, ("tensor", "sub"), axis=0, tiled=True),
        preferred_element_type=jnp.float32,
    )
    qkv = (qkv_total + qkv_bias[:, :, None]).astype(jnp.bfloat16)
    head_count = feature_share // HDIM
    qkv = qkv.reshape(3, head_count, HDIM, block_slots, block_len)
    same_window = window_ids[:, :, None] == window_ids[:, None, :]
    scores = jnp.einsum(
        "hdbi,hdbj->hbij", qkv[0], qkv[1], preferred_element_type=jnp.float32
    ) * HDIM ** (-0.5)
    scores = jnp.where(same_window[None], scores, -1e30)
    row_peak = jnp.max(scores, -1, keepdims=True)
    exponent = jnp.exp(scores - row_peak)
    attention_weights = (exponent / jnp.sum(exponent, -1, keepdims=True)).astype(jnp.bfloat16)
    context = jnp.einsum(
        "hbij,hdbj->hdbi", attention_weights, qkv[2], preferred_element_type=jnp.float32
    )
    context = context.astype(jnp.bfloat16).reshape(feature_share, local_cols)
    attn_out = lax.psum_scatter(
        jnp.einsum("hc,hn->cn", proj_weight, context, preferred_element_type=jnp.float32).astype(
            jnp.bfloat16
        ),
        ("tensor", "sub"),
        scatter_dimension=0,
        tiled=True,
    ).astype(jnp.float32)
    patch_out = (feats + attn_out + proj_bias[:, None]).astype(jnp.bfloat16)
    out_f = patch_out.astype(jnp.float32)
    merge_squares = lax.psum(jnp.sum(out_f * out_f, 0), ("tensor", "sub"))
    merge_in = (
        out_f * lax.rsqrt(merge_squares / vision_width + EPSILON)[None, :] * merge_gain[:, None]
    ).astype(jnp.bfloat16)
    merged = merge_in.reshape(feature_share, local_cols // 4, 4).transpose(2, 0, 1)
    merged_all = lax.all_gather(merged, "pool", axis=2, tiled=True)
    hidden_share = w1.shape[2]
    hidden_full = lax.psum(
        jnp.einsum("jfc,jfm->cm", w1, merged_all, preferred_element_type=jnp.float32).astype(
            jnp.bfloat16
        ),
        ("tensor", "sub"),
    ).astype(jnp.float32)
    bias_all = lax.all_gather(b1, ("tensor", "sub"), axis=0, tiled=True)
    bias_mine = lax.dynamic_slice_in_dim(bias_all, my_pool * hidden_share, hidden_share, 0)
    hidden = jax.nn.gelu(hidden_full + bias_mine[:, None], approximate=False).astype(jnp.bfloat16)
    block_total = block_route.shape[0]
    hidden_blocks = hidden.reshape(hidden_share, block_total, merged_rows)
    hot_groups = max(1, pool_count // 16)
    capacity_in = 2 * hot_groups + block_slots - 2
    pool_index = jnp.arange(pool_count, dtype=jnp.int32)
    goes = (block_route[None, :] == pool_index[:, None]).astype(jnp.int32)
    rank = jnp.cumsum(goes, 1) - goes
    slot_index = jnp.arange(capacity_in, dtype=jnp.int32)
    select = (
        (goes[:, None, :] == 1) & (rank[:, None, :] == slot_index[None, :, None])
    ).astype(jnp.bfloat16)
    routed = jnp.einsum(
        "qkn,fnr->fqkr", select, hidden_blocks, preferred_element_type=jnp.float32
    ).astype(jnp.bfloat16)
    routed = routed.reshape(hidden_share, pool_count, capacity_in * merged_rows)
    partial = jnp.einsum("hc,hqn->qcn", w2, routed, preferred_element_type=jnp.float32)
    projected = lax.psum_scatter(
        partial.astype(jnp.bfloat16), "pool", scatter_dimension=0, tiled=True
    )[0].astype(jnp.float32)
    count_mine = jnp.sum((block_route == my_pool).astype(jnp.int32))
    live_mask = (slot_index < count_mine).astype(jnp.float32)
    live_rows = jnp.broadcast_to(live_mask[:, None], (capacity_in, merged_rows)).reshape(-1)
    image_embeds = ((projected + b2[:, None]) * live_rows[None, :]).astype(jnp.bfloat16)
    embed_f = image_embeds.astype(jnp.float32)
    embed_squares = lax.psum(jnp.sum(embed_f * embed_f, 0), ("tensor", "sub"))
    normed_embeds = (
        embed_f
        * lax.rsqrt(embed_squares / (w2.shape[1] * groups) + EPSILON)[None, :]
        * llm_gain[:, None]
    ).astype(jnp.bfloat16)
    return (image_embeds, normed_embeds)


def fused_kernel(
    vision_width, model_width, patches, ids_row, routes, norm_gain, qkv_bias, proj_w, proj_bias,
    merge_gain, b1, b2, llm_gain, qkv_hbm, w1_hbm, w2_hbm,
    img, nrm, qkv_w, w1, w2, pw, fcols, lcols, id_col, picks, load_sem,
    xall, sall, pwall, gcol, xin, qkv, ctxall, zall, pbuf, rsib, csum, rx, hid, rt, obuf, rup, rdn,
    sq, sq2, acc_ref,
    x_send, x_recv, c_send, c_recv, s_send, s_recv, w_send, w_recv, q_send, q_recv,
    z_send, z_recv, h1_send, h1_recv, h2_send, h2_recv, h3_send, h3_recv,
    o_send, u_recv, d_recv, l_send, l_recv,
):
    f32, bf16 = jnp.float32, jnp.bfloat16
    feat, cols = patches.shape
    half_cols = cols // 2
    blocks, block_len = ids_row.shape
    heads = feat // HDIM
    share = w1.shape[2]
    hs = share // 2
    loads = [
        pltpu.make_async_copy(a, b, load_sem.at[k])
        for k, (a, b) in enumerate(((qkv_hbm, qkv_w), (w1_hbm, w1), (w2_hbm, w2)))
    ]
    for load in loads:
        load.start()
    p, tx, sc = lax.axis_index("pool"), lax.axis_index("tensor"), lax.axis_index("sub")
    me, xt, st, dt = tx * 2 + sc, (1 - tx) * 2 + sc, tx * 2 + 1 - sc, (1 - tx) * 2 + 1 - sc
    xp, sib, diag = {"tensor": 1 - tx}, {"sub": 1 - sc}, {"tensor": 1 - tx, "sub": 1 - sc}
    top = zall.shape[0] - 1

    def rcopy(src, dst, ss, rs, dev):
        return pltpu.make_async_remote_copy(
            src_ref=src, dst_ref=dst, send_sem=ss, recv_sem=rs, device_id=dev,
            device_id_type=pl.DeviceIdType.MESH,
        )

    barrier = pltpu.get_barrier_semaphore()
    for dev in (xp, sib, diag):
        pl.semaphore_signal(barrier, inc=1, device_id=dev, device_id_type=pl.DeviceIdType.MESH)

    @pl.when(p > 0)
    def _():
        pl.semaphore_signal(
            barrier, inc=1, device_id={"pool": p - 1}, device_id_type=pl.DeviceIdType.MESH
        )

    @pl.when(p < top)
    def _():
        pl.semaphore_signal(
            barrier, inc=1, device_id={"pool": p + 1}, device_id_type=pl.DeviceIdType.MESH
        )

    for pair in range(2):
        xall[pair, me] = patches[:, pair * half_cols : (pair + 1) * half_cols]
    base = sall.shape[2] - share
    sall[me, 0:1, :feat] = norm_gain[...]
    sall[me, 0:1, base:] = b1[...]
    pl.semaphore_wait(barrier, 3 + (p + top - 1) // top + (2 * top - p - 1) // top)

    def gather_start(buf, pair, ssem, rsem):
        own = buf.at[pair, me]
        rcopy(own, own, ssem.at[pair, 0], rsem.at[pair, me], xp).start()
        rcopy(own, own, ssem.at[pair, 1], rsem.at[pair, me], sib).start()

    def gather_finish(buf, pair, ssem, rsem):
        other = buf.at[pair, xt]
        fwd = rcopy(other, other, ssem.at[pair, 2], rsem.at[pair, xt], sib)
        fwd.wait_recv()
        fwd.start()
        for slot in (st, dt):
            rcopy(other, buf.at[pair, slot], ssem.at[pair, 2], rsem.at[pair, slot], sib).wait_recv()

    def gather_drain(buf, pair, ssem, rsem):
        for k in range(3):
            rcopy(buf.at[pair, me], buf.at[pair, me], ssem.at[pair, k], rsem.at[pair, me], sib).wait_send()

    peers = ((xp, xt), (sib, st), (diag, dt))
    for k, (dev, _t) in enumerate(peers):
        rcopy(sall.at[me], sall.at[me], s_send.at[k], s_recv.at[me], dev).start()
    gather_start(xall, 0, x_send, x_recv)
    gather_start(xall, 1, x_send, x_recv)
    for t in range(4):
        pw[t] = proj_w[:, t * feat : (t + 1) * feat]
    pwall[me] = pw[me]
    for k, (dev, t) in enumerate(peers):
        rcopy(pw.at[t], pwall.at[me], w_send.at[k], w_recv.at[me], dev).start()

    def to_column(row):
        size = row.shape[1]
        r = lax.broadcasted_iota(jnp.int32, (size, size), 0)
        c = lax.broadcasted_iota(jnp.int32, (size, size), 1)
        return jnp.sum(jnp.where(r == c, row, 0.0), 1, keepdims=True)

    for c in range(3):
        fcols[c] = to_column(qkv_bias[c : c + 1])
    fcols[3] = to_column(proj_bias[...])
    fcols[4] = to_column(merge_gain[...])
    for b in range(blocks):
        id_col[b] = to_column(ids_row[b : b + 1].astype(f32))
    pieces, piece = obuf.shape[1], obuf.shape[2]
    for r in range(pieces):
        lcols[0, r * piece : (r + 1) * piece] = to_column(b2[:, r * piece : (r + 1) * piece])
        lcols[1, r * piece : (r + 1) * piece] = to_column(llm_gain[:, r * piece : (r + 1) * piece])

    out_cols = img.shape[1]
    merged_rows = block_len // 4
    total_blocks = routes.shape[0]
    r_i = lax.broadcasted_iota(jnp.int32, (merged_rows, out_cols), 0)
    c_i = lax.broadcasted_iota(jnp.int32, (merged_rows, out_cols), 1)
    count = 0
    for n in range(total_blocks):
        route_n = routes[n]
        count += jnp.where(route_n == p, 1, 0)
        rank = 0
        for earlier in range(n):
            rank += jnp.where(routes[earlier] == route_n, 1, 0)
        first = jnp.where(
            rank < out_cols // merged_rows, route_n * out_cols + rank * merged_rows, -(1 << 20)
        )
        for q in range(top + 1):
            picks[q, n * merged_rows : (n + 1) * merged_rows] = jnp.where(
                r_i + (first - q * out_cols) == c_i, 1.0, 0.0
            ).astype(bf16)
    lane = lax.broadcasted_iota(jnp.int32, (1, out_cols), 1)
    live = jnp.where(lane < count * merged_rows, 1.0, 0.0)

    for k, (dev, t) in enumerate(peers):
        rcopy(sall.at[t], sall.at[t], s_send.at[k], s_recv.at[t], dev).wait_recv()

    for t in range(4):
        gcol[t] = to_column(sall[t, 0:1, :feat])
    loads[0].wait()

    def dot0(a, b):
        return lax.dot_general(a, b, (((0,), (0,)), ((), ())), preferred_element_type=f32)

    per_pair = blocks // 2
    for pair in range(2):
        gather_finish(xall, pair, x_send, x_recv)
        total = jnp.zeros((1, half_cols), f32)
        for t in range(4):
            v = xall[pair, t].astype(f32)
            total += jnp.sum(v * v, 0, keepdims=True)
        inv = lax.rsqrt(total / vision_width + EPSILON)
        for t in range(4):
            xin[t * feat : (t + 1) * feat] = (
                xall[pair, t].astype(f32) * inv * gcol[t]
            ).astype(bf16)
        for c in range(3):
            qkv[c] = (
                jnp.dot(qkv_w[c], xin[...], preferred_element_type=f32) + fcols[c]
            ).astype(bf16)
        for bb in range(per_pair):
            b = pair * per_pair + bb
            lo = bb * block_len
            same = id_col[b] == ids_row[b : b + 1, :].astype(f32)

            def head(h, carry):
                r = pl.ds(pl.multiple_of(h * HDIM, HDIM), HDIM)
                q = qkv[0, r, lo : lo + block_len]
                k = qkv[1, r, lo : lo + block_len]
                v = qkv[2, r, lo : lo + block_len]
                scores = jnp.where(same, dot0(k, q) * HDIM ** (-0.5), -1e30)
                e = jnp.exp(scores - jnp.max(scores, 0, keepdims=True))
                a = (e / jnp.sum(e, 0, keepdims=True)).astype(bf16)
                ctxall[pair, me, r, lo : lo + block_len] = jnp.dot(
                    v, a, preferred_element_type=f32
                ).astype(bf16)
                return carry

            lax.fori_loop(0, heads, head, 0)
        gather_start(ctxall, pair, c_send, c_recv)

    for k, (dev, t) in enumerate(peers):
        rcopy(pw.at[t], pwall.at[t], w_send.at[k], w_recv.at[t], dev).wait_recv()

    for pair in range(2):
        gather_finish(ctxall, pair, c_send, c_recv)
        total = patches[:, pair * half_cols : (pair + 1) * half_cols].astype(f32) + fcols[3]
        for t in range(4):
            total += (
                dot0(pwall[t], ctxall[pair, t])
                .astype(bf16)
                .astype(f32)
            )
        out = total.astype(bf16).astype(f32)
        sq[pair, me] = jnp.broadcast_to(jnp.sum(out * out, 0, keepdims=True), (8, half_cols))
        for k, (dev, t) in enumerate(peers):
            rcopy(sq.at[pair, me], sq.at[pair, me], q_send.at[pair, k], q_recv.at[pair, me], dev).start()
        for k, (dev, t) in enumerate(peers):
            rcopy(sq.at[pair, t], sq.at[pair, t], q_send.at[pair, k], q_recv.at[pair, t], dev).wait_recv()
        squares = sq[pair, 0, 0:1] + sq[pair, 1, 0:1] + sq[pair, 2, 0:1] + sq[pair, 3, 0:1]
        merge_in = (
            out * lax.rsqrt(squares / vision_width + EPSILON) * fcols[4]
        ).astype(bf16)
        n_i = lax.broadcasted_iota(jnp.int32, (half_cols, half_cols // 4), 0)
        m_i = lax.broadcasted_iota(jnp.int32, (half_cols, half_cols // 4), 1)
        for j in range(4):
            pick = jnp.where(n_i == 4 * m_i + j, 1.0, 0.0).astype(bf16)
            zall[p, pair, j] = jnp.dot(merge_in, pick, preferred_element_type=f32).astype(bf16)
        own = zall.at[p, pair]

        @pl.when(p < top)
        def _():
            rcopy(own, own, z_send.at[0, p, pair], z_recv.at[p, pair], {"pool": p + 1}).start()

        @pl.when(p > 0)
        def _():
            rcopy(own, own, z_send.at[1, p, pair], z_recv.at[p, pair], {"pool": p - 1}).start()

    b1_lo = sall[p, 0:1, base : base + hs]
    b1_hi = sall[p, 0:1, base + hs : base + share]
    b1_row = jnp.where(sc == 0, b1_lo, b1_hi)
    acc_ref[:hs, 0:1] = to_column(b1_row)
    loads[1].wait()

    places = 2 * top + 1
    width = half_cols // 4

    def place(k):
        pair, kk = k // places, k % places
        step = (kk + 1) // 2
        return pair, p + step * (1 - 2 * (kk % 2))

    def on_chunk(k, fn):
        pair, src = place(k)

        @pl.when((k >= 0) & (k < 2 * places) & (src >= 0) & (src <= top))
        def _():
            fn(pair, src)

    def step1(pair, src):
        chunk = zall.at[src, pair]

        @pl.when(src != p)
        def _():
            rcopy(chunk, chunk, z_send.at[0, src, pair], z_recv.at[src, pair], sib).wait_recv()

        @pl.when((src < p) & (p < top))
        def _():
            rcopy(chunk, chunk, z_send.at[0, src, pair], z_recv.at[src, pair], {"pool": p + 1}).start()

        @pl.when((src > p) & (p > 0))
        def _():
            rcopy(chunk, chunk, z_send.at[1, src, pair], z_recv.at[src, pair], {"pool": p - 1}).start()

        c = src * 2 + pair
        total = dot0(w1[0], zall[src, pair, 0])
        for j in range(1, 4):
            total += dot0(w1[j], zall[src, pair, j])
        pbuf[c, 0] = total[:hs].astype(bf16)
        pbuf[c, 1] = total[hs:].astype(bf16)
        rcopy(pbuf.at[c, 1 - sc], rsib.at[c], h1_send.at[c], h1_recv.at[c], sib).start()

    def step2(pair, src):
        c = src * 2 + pair
        rcopy(pbuf.at[c, 1 - sc], rsib.at[c], h1_send.at[c], h1_recv.at[c], sib).wait()
        csum[c] = (pbuf[c, sc].astype(f32) + rsib[c].astype(f32)).astype(bf16)
        rcopy(csum.at[c], rx.at[c], h2_send.at[c], h2_recv.at[c], xp).start()

    def hid_copy(c):
        dst = hid.at[sc, :, pl.ds(pl.multiple_of(c * width, width), width)]
        return rcopy(dst, dst, h3_send.at[c], h3_recv.at[c], sib)

    def step3(pair, src):
        c = src * 2 + pair
        rcopy(csum.at[c], rx.at[c], h2_send.at[c], h2_recv.at[c], xp).wait()
        pre = csum[c].astype(f32) + rx[c].astype(f32) + acc_ref[:hs, 0:1]
        act = 0.5 * pre * (1.0 + lax.erf(pre * (0.5**0.5)))
        hid[sc, :, pl.ds(pl.multiple_of(c * width, width), width)] = act.astype(bf16)
        hid_copy(c).start()

    def hidden_step(k, carry):
        on_chunk(k, step1)
        on_chunk(k - 1, step2)
        on_chunk(k - 2, step3)
        return carry

    lax.fori_loop(0, 2 * places + 2, hidden_step, 0)

    def hid_wait(c, carry):
        hid_copy(c).wait_send()
        other = hid.at[1 - sc, :, pl.ds(pl.multiple_of(c * width, width), width)]
        rcopy(other, other, h3_send.at[c], h3_recv.at[c], sib).wait_recv()
        return carry

    lax.fori_loop(0, 2 * (top + 1), hid_wait, 0)

    loads[2].wait()

    def route(q, carry):
        for half in range(2):
            rt[q, half * hs : (half + 1) * hs] = jnp.dot(
                hid[half], picks[q], preferred_element_type=f32
            ).astype(bf16)
        return carry

    lax.fori_loop(0, top + 1, route, 0)

    def part(q, r):
        return dot0(w2[:, pl.ds(pl.multiple_of(r * piece, piece), piece)], rt[q])

    def send_one(q, r, buf, sem, dev, has_more, from_dev):
        acc_ref[...] = part(q, r)

        @pl.when(has_more)
        def _():
            rcopy(obuf.at[q, r], buf.at[q, r], o_send.at[q, r], sem.at[q, r], from_dev).wait_recv()
            acc_ref[...] += buf[q, r].astype(f32)

        obuf[q, r] = acc_ref[...].astype(bf16)
        rcopy(obuf.at[q, r], buf.at[q, r], o_send.at[q, r], sem.at[q, r], dev).start()

    def out_step(k, carry):
        delta, r = top - k // pieces, k % pieces

        @pl.when(p + delta <= top)
        def _():
            send_one(p + delta, r, rup, u_recv, {"pool": p + 1}, p > 0, sib)

        @pl.when(p - delta >= 0)
        def _():
            send_one(p - delta, r, rdn, d_recv, {"pool": p - 1}, p < top, sib)

        return carry

    lax.fori_loop(0, top * pieces, out_step, 0)

    def last_step(r, squares):
        rr = pl.ds(pl.multiple_of(r * piece, piece), piece)
        acc_ref[...] = part(p, r) + lcols[0, rr]

        @pl.when(p > 0)
        def _():
            rcopy(obuf.at[p, r], rup.at[p, r], o_send.at[p, r], u_recv.at[p, r], sib).wait_recv()
            acc_ref[...] += rup[p, r].astype(f32)

        @pl.when(p < top)
        def _():
            rcopy(obuf.at[p, r], rdn.at[p, r], o_send.at[p, r], d_recv.at[p, r], sib).wait_recv()
            acc_ref[...] += rdn[p, r].astype(f32)

        res = (acc_ref[...] * live).astype(bf16)
        img[rr, :] = res
        res = res.astype(f32)
        return squares + jnp.sum(res * res, 0, keepdims=True)

    squares = lax.fori_loop(0, pieces, last_step, jnp.zeros((1, out_cols), f32))
    sq2[me] = jnp.broadcast_to(squares, (8, out_cols))
    for k, (dev, t) in enumerate(peers):
        rcopy(sq2.at[me], sq2.at[me], l_send.at[k], l_recv.at[me], dev).start()

    for pair in range(2):
        gather_drain(xall, pair, x_send, x_recv)
        gather_drain(ctxall, pair, c_send, c_recv)
        for k in range(3):
            rcopy(sq.at[pair, me], sq.at[pair, me], q_send.at[pair, k], q_recv.at[pair, me], sib).wait_send()
        for src in range(top + 1):
            chunk = zall.at[src, pair]

            @pl.when((src <= p) & (p < top))
            def _():
                rcopy(chunk, chunk, z_send.at[0, src, pair], z_recv.at[src, pair], sib).wait_send()

            @pl.when((src >= p) & (p > 0))
            def _():
                rcopy(chunk, chunk, z_send.at[1, src, pair], z_recv.at[src, pair], sib).wait_send()

    for k in range(3):
        rcopy(sall.at[me], sall.at[me], s_send.at[k], s_recv.at[me], sib).wait_send()
        rcopy(pw.at[me], pwall.at[me], w_send.at[k], w_recv.at[me], sib).wait_send()
    for q in range(top + 1):

        @pl.when(q != p)
        def _():
            for r in range(pieces):
                rcopy(obuf.at[q, r], rup.at[q, r], o_send.at[q, r], u_recv.at[q, r], sib).wait_send()

    for k, (dev, t) in enumerate(peers):
        rcopy(sq2.at[t], sq2.at[t], l_send.at[k], l_recv.at[t], dev).wait()
    squares = sq2[0, 0:1] + sq2[1, 0:1] + sq2[2, 0:1] + sq2[3, 0:1]
    inv = lax.rsqrt(squares / model_width + EPSILON)

    def norm_step(r, carry):
        rr = pl.ds(pl.multiple_of(r * piece, piece), piece)
        nrm[rr, :] = (img[rr, :].astype(f32) * inv * lcols[1, rr]).astype(bf16)
        return carry

    lax.fori_loop(0, pieces, norm_step, 0)


def fused_shards(
    patches, window_ids, block_route, norm_gain, qkv_weight, qkv_bias, proj_weight, proj_bias,
    merge_gain, w1, b1, w2, b2, llm_gain,
):
    f32, bf16 = jnp.float32, jnp.bfloat16
    feat, cols = patches.shape
    pool = lax.axis_size("pool")
    slots, block_len = window_ids.shape
    width = qkv_weight.shape[1]
    merged_rows = block_len // 4
    hot_groups = max(1, pool // 16)
    capacity = 2 * hot_groups + slots - 2
    out_cols = capacity * merged_rows
    share = w1.shape[2]
    pad = -feat % 128
    row_len = feat + pad + share
    local_out = w2.shape[1]
    hc, hs, wd = cols // 2, share // 2, cols // 8
    n2 = 2 * pool
    pieces = 4
    piece = local_out // pieces
    V, D = pltpu.VMEM, pltpu.SemaphoreType.DMA
    total = block_route.shape[0]
    scratch = [
        V((3, feat, width), bf16), V(w1.shape, bf16), V(w2.shape, bf16), V((4, feat, feat), bf16),
        V((5, feat, 1), f32), V((2, local_out, 1), f32), V((slots, block_len, 1), f32),
        V((pool, total * merged_rows, out_cols), bf16), D((3,)),
        V((2, 4, feat, hc), bf16), V((4, 8, row_len), f32), V((4, feat, feat), bf16),
        V((4, feat, 1), f32), V((width, hc), bf16), V((3, feat, hc), bf16),
        V((2, 4, feat, hc), bf16), V((pool, 2, 4, feat, wd), bf16), V((n2, 2, hs, wd), bf16),
        V((n2, hs, wd), bf16), V((n2, hs, wd), bf16), V((n2, hs, wd), bf16),
        V((2, hs, n2 * wd), bf16), V((pool, share, out_cols), bf16),
        V((pool, pieces, piece, out_cols), bf16), V((pool, pieces, piece, out_cols), bf16),
        V((pool, pieces, piece, out_cols), bf16),
        V((2, 4, 8, hc), f32), V((4, 8, out_cols), f32), V((piece, out_cols), f32),
        D((2, 3)), D((2, 4)), D((2, 3)), D((2, 4)), D((3,)), D((4,)), D((3,)), D((4,)),
        D((2, 3)), D((2, 4)), D((2, pool, 2)), D((pool, 2)),
        D((n2,)), D((n2,)), D((n2,)), D((n2,)), D((n2,)), D((n2,)),
        D((pool, pieces)), D((pool, pieces)), D((pool, pieces)), D((3,)), D((4,)),
    ]
    shape = jax.ShapeDtypeStruct((local_out, out_cols), bf16)
    vm = pl.BlockSpec(memory_space=pltpu.VMEM)
    return pl.pallas_call(
        functools.partial(fused_kernel, width, local_out * 4),
        out_shape=(shape, shape),
        in_specs=[vm, vm, pl.BlockSpec(memory_space=pltpu.SMEM)]
        + [vm] * 8
        + [pl.BlockSpec(memory_space=pl.ANY)] * 3,
        out_specs=(vm, vm),
        scratch_shapes=scratch,
        compiler_params=pltpu.CompilerParams(
            collective_id=0, has_side_effects=True, vmem_limit_bytes=60 << 20
        ),
        name="vision_fused",
    )(
        patches, window_ids, block_route, norm_gain[None, :], qkv_bias, proj_weight,
        proj_bias[None, :], merge_gain[None, :], b1[None, :], b2[None, :], llm_gain[None, :],
        qkv_weight.transpose(0, 2, 1), w1, w2,
    )


def fused_fits(mesh):
    return mesh.shape["tensor"] == 2 and mesh.shape["sub"] == 2 and mesh.shape["pool"] == 4


def solution(mesh):
    placed = (
        P(("tensor", "sub"), ("groups", "pool")),
        P(("groups", "pool"), None),
        P("groups"),
        P(("tensor", "sub")),
        P(None, None, ("tensor", "sub")),
        P(None, ("tensor", "sub")),
        P(("tensor", "sub"), None),
        P(("tensor", "sub")),
        P(("tensor", "sub")),
        P(None, ("tensor", "sub"), "pool"),
        P(("tensor", "sub")),
        P("pool", ("tensor", "sub")),
        P(("tensor", "sub")),
        P(("tensor", "sub")),
    )
    return jax.shard_map(
        fused_shards if fused_fits(mesh) else shards,
        mesh=mesh,
        in_specs=placed,
        out_specs=(
            P(("tensor", "sub"), ("groups", "pool")),
            P(("tensor", "sub"), ("groups", "pool")),
        ),
        check_vma=False,
    )
```

```python
import functools

import jax
import jax.numpy as jnp
from jax import lax
from jax.experimental import pallas as pl
from jax.experimental.pallas import tpu as pltpu
from jax.sharding import PartitionSpec as P

HDIM = 80


EPSILON = 1e-06


def shards(
    patches,
    window_ids,
    block_route,
    norm_gain,
    qkv_weight,
    qkv_bias,
    proj_weight,
    proj_bias,
    merge_gain,
    w1,
    b1,
    w2,
    b2,
    llm_gain,
):
    feature_share, local_cols = patches.shape
    vision_width = qkv_weight.shape[1]
    groups = lax.axis_size(("tensor", "sub"))
    pool_count = lax.axis_size("pool")
    my_pool = lax.axis_index("pool")
    block_slots, block_len = window_ids.shape
    merged_rows = block_len // 4
    feats = patches.astype(jnp.float32)
    squares = lax.psum(jnp.sum(feats * feats, 0), ("tensor", "sub"))
    patch_in = (
        feats * lax.rsqrt(squares / vision_width + EPSILON)[None, :] * norm_gain[:, None]
    ).astype(jnp.bfloat16)
    weight_rows = qkv_weight
    qkv_total = jnp.einsum(
        "cio,in->con",
        weight_rows,
        lax.all_gather(patch_in, ("tensor", "sub"), axis=0, tiled=True),
        preferred_element_type=jnp.float32,
    )
    qkv = (qkv_total + qkv_bias[:, :, None]).astype(jnp.bfloat16)
    head_count = feature_share // HDIM
    qkv = qkv.reshape(3, head_count, HDIM, block_slots, block_len)
    same_window = window_ids[:, :, None] == window_ids[:, None, :]
    scores = jnp.einsum(
        "hdbi,hdbj->hbij", qkv[0], qkv[1], preferred_element_type=jnp.float32
    ) * HDIM ** (-0.5)
    scores = jnp.where(same_window[None], scores, -1e30)
    row_peak = jnp.max(scores, -1, keepdims=True)
    exponent = jnp.exp(scores - row_peak)
    attention_weights = (exponent / jnp.sum(exponent, -1, keepdims=True)).astype(jnp.bfloat16)
    context = jnp.einsum(
        "hbij,hdbj->hdbi", attention_weights, qkv[2], preferred_element_type=jnp.float32
    )
    context = context.astype(jnp.bfloat16).reshape(feature_share, local_cols)
    attn_out = lax.psum_scatter(
        jnp.einsum("hc,hn->cn", proj_weight, context, preferred_element_type=jnp.float32).astype(
            jnp.bfloat16
        ),
        ("tensor", "sub"),
        scatter_dimension=0,
        tiled=True,
    ).astype(jnp.float32)
    patch_out = (feats + attn_out + proj_bias[:, None]).astype(jnp.bfloat16)
    out_f = patch_out.astype(jnp.float32)
    merge_squares = lax.psum(jnp.sum(out_f * out_f, 0), ("tensor", "sub"))
    merge_in = (
        out_f * lax.rsqrt(merge_squares / vision_width + EPSILON)[None, :] * merge_gain[:, None]
    ).astype(jnp.bfloat16)
    merged = merge_in.reshape(feature_share, local_cols // 4, 4).transpose(2, 0, 1)
    merged_all = lax.all_gather(merged, "pool", axis=2, tiled=True)
    hidden_share = w1.shape[2]
    hidden_full = lax.psum(
        jnp.einsum("jfc,jfm->cm", w1, merged_all, preferred_element_type=jnp.float32).astype(
            jnp.bfloat16
        ),
        ("tensor", "sub"),
    ).astype(jnp.float32)
    bias_all = lax.all_gather(b1, ("tensor", "sub"), axis=0, tiled=True)
    bias_mine = lax.dynamic_slice_in_dim(bias_all, my_pool * hidden_share, hidden_share, 0)
    hidden = jax.nn.gelu(hidden_full + bias_mine[:, None], approximate=False).astype(jnp.bfloat16)
    block_total = block_route.shape[0]
    hidden_blocks = hidden.reshape(hidden_share, block_total, merged_rows)
    hot_groups = max(1, pool_count // 16)
    capacity_in = 2 * hot_groups + block_slots - 2
    pool_index = jnp.arange(pool_count, dtype=jnp.int32)
    goes = (block_route[None, :] == pool_index[:, None]).astype(jnp.int32)
    rank = jnp.cumsum(goes, 1) - goes
    slot_index = jnp.arange(capacity_in, dtype=jnp.int32)
    select = (
        (goes[:, None, :] == 1) & (rank[:, None, :] == slot_index[None, :, None])
    ).astype(jnp.bfloat16)
    routed = jnp.einsum(
        "qkn,fnr->fqkr", select, hidden_blocks, preferred_element_type=jnp.float32
    ).astype(jnp.bfloat16)
    routed = routed.reshape(hidden_share, pool_count, capacity_in * merged_rows)
    partial = jnp.einsum("hc,hqn->qcn", w2, routed, preferred_element_type=jnp.float32)
    projected = lax.psum_scatter(
        partial.astype(jnp.bfloat16), "pool", scatter_dimension=0, tiled=True
    )[0].astype(jnp.float32)
    count_mine = jnp.sum((block_route == my_pool).astype(jnp.int32))
    live_mask = (slot_index < count_mine).astype(jnp.float32)
    live_rows = jnp.broadcast_to(live_mask[:, None], (capacity_in, merged_rows)).reshape(-1)
    image_embeds = ((projected + b2[:, None]) * live_rows[None, :]).astype(jnp.bfloat16)
    embed_f = image_embeds.astype(jnp.float32)
    embed_squares = lax.psum(jnp.sum(embed_f * embed_f, 0), ("tensor", "sub"))
    normed_embeds = (
        embed_f
        * lax.rsqrt(embed_squares / (w2.shape[1] * groups) + EPSILON)[None, :]
        * llm_gain[:, None]
    ).astype(jnp.bfloat16)
    return (image_embeds, normed_embeds)


def fused_kernel(
    vision_width, model_width, patches, ids_row, routes, norm_gain, qkv_bias, proj_w, proj_bias,
    merge_gain, b1, b2, llm_gain, qkv_hbm, w1_hbm, w2_hbm,
    img, nrm, qkv_w, w1, w2, pw, fcols, lcols, id_col, picks, load_sem,
    xall, sall, pwall, gcol, xin, qkv, ctxall, zall, pbuf, rsib, csum, rx, hid, rt, obuf, rup, rdn,
    sq, sq2, acc_ref,
    x_send, x_recv, c_send, c_recv, s_send, s_recv, w_send, w_recv, q_send, q_recv,
    z_send, z_recv, h1_send, h1_recv, h2_send, h2_recv, h3_send, h3_recv,
    o_send, u_recv, d_recv, l_send, l_recv,
):
    f32, bf16 = jnp.float32, jnp.bfloat16
    feat, cols = patches.shape
    half_cols = cols // 2
    blocks, block_len = ids_row.shape
    heads = feat // HDIM
    share = w1.shape[2]
    hs = share // 2
    loads = [
        pltpu.make_async_copy(a, b, load_sem.at[k])
        for k, (a, b) in enumerate(((qkv_hbm, qkv_w), (w1_hbm, w1), (w2_hbm, w2)))
    ]
    for load in loads:
        load.start()
    p, tx, sc = lax.axis_index("pool"), lax.axis_index("tensor"), lax.axis_index("sub")
    me, xt, st, dt = tx * 2 + sc, (1 - tx) * 2 + sc, tx * 2 + 1 - sc, (1 - tx) * 2 + 1 - sc
    xp, sib, diag = {"tensor": 1 - tx}, {"sub": 1 - sc}, {"tensor": 1 - tx, "sub": 1 - sc}
    top = zall.shape[0] - 1

    def rcopy(src, dst, ss, rs, dev):
        return pltpu.make_async_remote_copy(
            src_ref=src, dst_ref=dst, send_sem=ss, recv_sem=rs, device_id=dev,
            device_id_type=pl.DeviceIdType.MESH,
        )

    barrier = pltpu.get_barrier_semaphore()
    for dev in (xp, sib, diag):
        pl.semaphore_signal(barrier, inc=1, device_id=dev, device_id_type=pl.DeviceIdType.MESH)

    @pl.when(p > 0)
    def _():
        pl.semaphore_signal(
            barrier, inc=1, device_id={"pool": p - 1}, device_id_type=pl.DeviceIdType.MESH
        )

    @pl.when(p < top)
    def _():
        pl.semaphore_signal(
            barrier, inc=1, device_id={"pool": p + 1}, device_id_type=pl.DeviceIdType.MESH
        )

    for pair in range(2):
        xall[pair, me] = patches[:, pair * half_cols : (pair + 1) * half_cols]
    base = sall.shape[2] - share
    sall[me, 0:1, :feat] = norm_gain[...][None, :]
    sall[me, 0:1, base:] = b1[...][None, :]
    pl.semaphore_wait(barrier, 3 + (p + top - 1) // top + (2 * top - p - 1) // top)

    def gather_start(buf, pair, ssem, rsem):
        own = buf.at[pair, me]
        rcopy(own, own, ssem.at[pair, 0], rsem.at[pair, me], xp).start()
        rcopy(own, own, ssem.at[pair, 1], rsem.at[pair, me], sib).start()

    def gather_finish(buf, pair, ssem, rsem):
        other = buf.at[pair, xt]
        fwd = rcopy(other, other, ssem.at[pair, 2], rsem.at[pair, xt], sib)
        fwd.wait_recv()
        fwd.start()
        for slot in (st, dt):
            rcopy(other, buf.at[pair, slot], ssem.at[pair, 2], rsem.at[pair, slot], sib).wait_recv()

    def gather_drain(buf, pair, ssem, rsem):
        for k in range(3):
            rcopy(buf.at[pair, me], buf.at[pair, me], ssem.at[pair, k], rsem.at[pair, me], sib).wait_send()

    peers = ((xp, xt), (sib, st), (diag, dt))
    for k, (dev, _t) in enumerate(peers):
        rcopy(sall.at[me], sall.at[me], s_send.at[k], s_recv.at[me], dev).start()
    gather_start(xall, 0, x_send, x_recv)
    gather_start(xall, 1, x_send, x_recv)
    for t in range(4):
        pw[t] = proj_w[:, t * feat : (t + 1) * feat]
    pwall[me] = pw[me]
    for k, (dev, t) in enumerate(peers):
        rcopy(pw.at[t], pwall.at[me], w_send.at[k], w_recv.at[me], dev).start()

    def to_column(row):
        size = row.shape[1]
        r = lax.broadcasted_iota(jnp.int32, (size, size), 0)
        c = lax.broadcasted_iota(jnp.int32, (size, size), 1)
        return jnp.sum(jnp.where(r == c, row, 0.0), 1, keepdims=True)

    for c in range(3):
        fcols[c] = to_column(qkv_bias[c : c + 1])
    fcols[3] = to_column(proj_bias[...][None, :])
    fcols[4] = to_column(merge_gain[...][None, :])
    for b in range(blocks):
        id_col[b] = to_column(ids_row[b : b + 1].astype(f32))
    pieces, piece = obuf.shape[1], obuf.shape[2]
    for r in range(pieces):
        lcols[0, r * piece : (r + 1) * piece] = to_column(b2[:, r * piece : (r + 1) * piece])
        lcols[1, r * piece : (r + 1) * piece] = to_column(llm_gain[:, r * piece : (r + 1) * piece])

    out_cols = img.shape[1]
    merged_rows = block_len // 4
    total_blocks = routes.shape[0]
    r_i = lax.broadcasted_iota(jnp.int32, (merged_rows, out_cols), 0)
    c_i = lax.broadcasted_iota(jnp.int32, (merged_rows, out_cols), 1)
    count = 0
    for n in range(total_blocks):
        route_n = routes[n]
        count += jnp.where(route_n == p, 1, 0)
        rank = 0
        for earlier in range(n):
            rank += jnp.where(routes[earlier] == route_n, 1, 0)
        first = jnp.where(
            rank < out_cols // merged_rows, route_n * out_cols + rank * merged_rows, -(1 << 20)
        )
        for q in range(top + 1):
            picks[q, n * merged_rows : (n + 1) * merged_rows] = jnp.where(
                r_i + (first - q * out_cols) == c_i, 1.0, 0.0
            ).astype(bf16)
    lane = lax.broadcasted_iota(jnp.int32, (1, out_cols), 1)
    live = jnp.where(lane < count * merged_rows, 1.0, 0.0)

    for k, (dev, t) in enumerate(peers):
        rcopy(sall.at[t], sall.at[t], s_send.at[k], s_recv.at[t], dev).wait_recv()

    for t in range(4):
        gcol[t] = to_column(sall[t, 0:1, :feat])
    loads[0].wait()

    def dot0(a, b):
        return lax.dot_general(a, b, (((0,), (0,)), ((), ())), preferred_element_type=f32)

    per_pair = blocks // 2
    for pair in range(2):
        gather_finish(xall, pair, x_send, x_recv)
        total = jnp.zeros((1, half_cols), f32)
        for t in range(4):
            v = xall[pair, t].astype(f32)
            total += jnp.sum(v * v, 0, keepdims=True)
        inv = lax.rsqrt(total / vision_width + EPSILON)
        for t in range(4):
            xin[t * feat : (t + 1) * feat] = (
                xall[pair, t].astype(f32) * inv * gcol[t]
            ).astype(bf16)
        for c in range(3):
            qkv[c] = (
                jnp.dot(qkv_w[c], xin[...], preferred_element_type=f32) + fcols[c]
            ).astype(bf16)
        for bb in range(per_pair):
            b = pair * per_pair + bb
            lo = bb * block_len
            same = id_col[b] == ids_row[b : b + 1, :].astype(f32)

            def head(h, carry):
                r = pl.ds(pl.multiple_of(h * HDIM, HDIM), HDIM)
                q = qkv[0, r, lo : lo + block_len]
                k = qkv[1, r, lo : lo + block_len]
                v = qkv[2, r, lo : lo + block_len]
                scores = jnp.where(same, dot0(k, q) * HDIM ** (-0.5), -1e30)
                e = jnp.exp(scores - jnp.max(scores, 0, keepdims=True))
                a = (e * (1.0 / jnp.sum(e, 0, keepdims=True))).astype(bf16)
                ctxall[pair, me, r, lo : lo + block_len] = jnp.dot(
                    v, a, preferred_element_type=f32
                ).astype(bf16)
                return carry

            lax.fori_loop(0, heads, head, 0, unroll=True)
        gather_start(ctxall, pair, c_send, c_recv)

    for k, (dev, t) in enumerate(peers):
        rcopy(pw.at[t], pwall.at[t], w_send.at[k], w_recv.at[t], dev).wait_recv()

    for pair in range(2):
        gather_finish(ctxall, pair, c_send, c_recv)
        total = patches[:, pair * half_cols : (pair + 1) * half_cols].astype(f32) + fcols[3]
        for t in range(4):
            total += (
                dot0(pwall[t], ctxall[pair, t])
                .astype(bf16)
                .astype(f32)
            )
        out = total.astype(bf16).astype(f32)
        sq[pair, me] = jnp.broadcast_to(jnp.sum(out * out, 0, keepdims=True), (8, half_cols))
        for k, (dev, t) in enumerate(peers):
            rcopy(sq.at[pair, me], sq.at[pair, me], q_send.at[pair, k], q_recv.at[pair, me], dev).start()
        for k, (dev, t) in enumerate(peers):
            rcopy(sq.at[pair, t], sq.at[pair, t], q_send.at[pair, k], q_recv.at[pair, t], dev).wait_recv()
        squares = sq[pair, 0, 0:1] + sq[pair, 1, 0:1] + sq[pair, 2, 0:1] + sq[pair, 3, 0:1]
        merge_in = (
            out * lax.rsqrt(squares / vision_width + EPSILON) * fcols[4]
        ).astype(bf16)
        n_i = lax.broadcasted_iota(jnp.int32, (half_cols, half_cols // 4), 0)
        m_i = lax.broadcasted_iota(jnp.int32, (half_cols, half_cols // 4), 1)
        for j in range(4):
            pick = jnp.where(n_i == 4 * m_i + j, 1.0, 0.0).astype(bf16)
            zall[p, pair, j] = jnp.dot(merge_in, pick, preferred_element_type=f32).astype(bf16)
        own = zall.at[p, pair]

        @pl.when(p < top)
        def _():
            rcopy(own, own, z_send.at[0, p, pair], z_recv.at[p, pair], {"pool": p + 1}).start()

        @pl.when(p > 0)
        def _():
            rcopy(own, own, z_send.at[1, p, pair], z_recv.at[p, pair], {"pool": p - 1}).start()

    b1_lo = sall[p, 0:1, base : base + hs]
    b1_hi = sall[p, 0:1, base + hs : base + share]
    b1_row = jnp.where(sc == 0, b1_lo, b1_hi)
    acc_ref[:hs, 0:1] = to_column(b1_row)
    loads[1].wait()

    places = 2 * top + 1
    width = half_cols // 4

    def place(k):
        pair, kk = k // places, k % places
        step = (kk + 1) // 2
        return pair, p + step * (1 - 2 * (kk % 2))

    def on_chunk(k, fn):
        pair, src = place(k)

        @pl.when((k >= 0) & (k < 2 * places) & (src >= 0) & (src <= top))
        def _():
            fn(pair, src)

    def step1(pair, src):
        chunk = zall.at[src, pair]

        @pl.when(src != p)
        def _():
            rcopy(chunk, chunk, z_send.at[0, src, pair], z_recv.at[src, pair], sib).wait_recv()

        @pl.when((src < p) & (p < top))
        def _():
            rcopy(chunk, chunk, z_send.at[0, src, pair], z_recv.at[src, pair], {"pool": p + 1}).start()

        @pl.when((src > p) & (p > 0))
        def _():
            rcopy(chunk, chunk, z_send.at[1, src, pair], z_recv.at[src, pair], {"pool": p - 1}).start()

        c = src * 2 + pair
        total = dot0(w1[0], zall[src, pair, 0])
        for j in range(1, 4):
            total += dot0(w1[j], zall[src, pair, j])
        pbuf[c, 0] = total[:hs].astype(bf16)
        pbuf[c, 1] = total[hs:].astype(bf16)
        rcopy(pbuf.at[c, 1 - sc], rsib.at[c], h1_send.at[c], h1_recv.at[c], sib).start()

    def step2(pair, src):
        c = src * 2 + pair
        rcopy(pbuf.at[c, 1 - sc], rsib.at[c], h1_send.at[c], h1_recv.at[c], sib).wait()
        csum[c] = (pbuf[c, sc].astype(f32) + rsib[c].astype(f32)).astype(bf16)
        rcopy(csum.at[c], rx.at[c], h2_send.at[c], h2_recv.at[c], xp).start()

    def hid_copy(c):
        dst = hid.at[sc, :, pl.ds(pl.multiple_of(c * width, width), width)]
        return rcopy(dst, dst, h3_send.at[c], h3_recv.at[c], sib)

    def step3(pair, src):
        c = src * 2 + pair
        rcopy(csum.at[c], rx.at[c], h2_send.at[c], h2_recv.at[c], xp).wait()
        pre = csum[c].astype(f32) + rx[c].astype(f32) + acc_ref[:hs, 0:1]
        act = 0.5 * pre * (1.0 + lax.erf(pre * (0.5**0.5)))
        hid[sc, :, pl.ds(pl.multiple_of(c * width, width), width)] = act.astype(bf16)
        hid_copy(c).start()

    def hidden_step(k, carry):
        on_chunk(k, step1)
        on_chunk(k - 1, step2)
        on_chunk(k - 2, step3)
        return carry

    lax.fori_loop(0, 2 * places + 2, hidden_step, 0)

    def hid_wait(c, carry):
        hid_copy(c).wait_send()
        other = hid.at[1 - sc, :, pl.ds(pl.multiple_of(c * width, width), width)]
        rcopy(other, other, h3_send.at[c], h3_recv.at[c], sib).wait_recv()
        return carry

    lax.fori_loop(0, 2 * (top + 1), hid_wait, 0)

    loads[2].wait()

    def route(q, carry):
        for half in range(2):
            rt[q, half * hs : (half + 1) * hs] = jnp.dot(
                hid[half], picks[q], preferred_element_type=f32
            ).astype(bf16)
        return carry

    lax.fori_loop(0, top + 1, route, 0)

    def part(q, r):
        return dot0(w2[:, pl.ds(pl.multiple_of(r * piece, piece), piece)], rt[q])

    def send_one(q, r, buf, sem, dev, has_more, from_dev):
        acc_ref[...] = part(q, r)

        @pl.when(has_more)
        def _():
            rcopy(obuf.at[q, r], buf.at[q, r], o_send.at[q, r], sem.at[q, r], from_dev).wait_recv()
            acc_ref[...] += buf[q, r].astype(f32)

        obuf[q, r] = acc_ref[...].astype(bf16)
        rcopy(obuf.at[q, r], buf.at[q, r], o_send.at[q, r], sem.at[q, r], dev).start()

    def out_step(k, carry):
        delta, r = top - k // pieces, k % pieces

        @pl.when(p + delta <= top)
        def _():
            send_one(p + delta, r, rup, u_recv, {"pool": p + 1}, p > 0, sib)

        @pl.when(p - delta >= 0)
        def _():
            send_one(p - delta, r, rdn, d_recv, {"pool": p - 1}, p < top, sib)

        return carry

    lax.fori_loop(0, top * pieces, out_step, 0)

    def last_step(r, squares):
        rr = pl.ds(pl.multiple_of(r * piece, piece), piece)
        acc_ref[...] = part(p, r) + lcols[0, rr]

        @pl.when(p > 0)
        def _():
            rcopy(obuf.at[p, r], rup.at[p, r], o_send.at[p, r], u_recv.at[p, r], sib).wait_recv()
            acc_ref[...] += rup[p, r].astype(f32)

        @pl.when(p < top)
        def _():
            rcopy(obuf.at[p, r], rdn.at[p, r], o_send.at[p, r], d_recv.at[p, r], sib).wait_recv()
            acc_ref[...] += rdn[p, r].astype(f32)

        res = (acc_ref[...] * live).astype(bf16)
        img[rr, :] = res
        res = res.astype(f32)
        return squares + jnp.sum(res * res, 0, keepdims=True)

    squares = lax.fori_loop(0, pieces, last_step, jnp.zeros((1, out_cols), f32))
    sq2[me] = jnp.broadcast_to(squares, (8, out_cols))
    for k, (dev, t) in enumerate(peers):
        rcopy(sq2.at[me], sq2.at[me], l_send.at[k], l_recv.at[me], dev).start()

    for pair in range(2):
        gather_drain(xall, pair, x_send, x_recv)
        gather_drain(ctxall, pair, c_send, c_recv)
        for k in range(3):
            rcopy(sq.at[pair, me], sq.at[pair, me], q_send.at[pair, k], q_recv.at[pair, me], sib).wait_send()
        for src in range(top + 1):
            chunk = zall.at[src, pair]

            @pl.when((src <= p) & (p < top))
            def _():
                rcopy(chunk, chunk, z_send.at[0, src, pair], z_recv.at[src, pair], sib).wait_send()

            @pl.when((src >= p) & (p > 0))
            def _():
                rcopy(chunk, chunk, z_send.at[1, src, pair], z_recv.at[src, pair], sib).wait_send()

    for k in range(3):
        rcopy(sall.at[me], sall.at[me], s_send.at[k], s_recv.at[me], sib).wait_send()
        rcopy(pw.at[me], pwall.at[me], w_send.at[k], w_recv.at[me], sib).wait_send()
    for q in range(top + 1):

        @pl.when(q != p)
        def _():
            for r in range(pieces):
                rcopy(obuf.at[q, r], rup.at[q, r], o_send.at[q, r], u_recv.at[q, r], sib).wait_send()

    for k, (dev, t) in enumerate(peers):
        rcopy(sq2.at[t], sq2.at[t], l_send.at[k], l_recv.at[t], dev).wait()
    squares = sq2[0, 0:1] + sq2[1, 0:1] + sq2[2, 0:1] + sq2[3, 0:1]
    inv = lax.rsqrt(squares / model_width + EPSILON)

    def norm_step(r, carry):
        rr = pl.ds(pl.multiple_of(r * piece, piece), piece)
        nrm[rr, :] = (img[rr, :].astype(f32) * inv * lcols[1, rr]).astype(bf16)
        return carry

    lax.fori_loop(0, pieces, norm_step, 0)


def fused_shards(
    patches, window_ids, block_route, norm_gain, qkv_weight, qkv_bias, proj_weight, proj_bias,
    merge_gain, w1, b1, w2, b2, llm_gain,
):
    f32, bf16 = jnp.float32, jnp.bfloat16
    feat, cols = patches.shape
    pool = lax.axis_size("pool")
    slots, block_len = window_ids.shape
    width = qkv_weight.shape[1]
    merged_rows = block_len // 4
    hot_groups = max(1, pool // 16)
    capacity = 2 * hot_groups + slots - 2
    out_cols = capacity * merged_rows
    share = w1.shape[2]
    pad = -feat % 128
    row_len = feat + pad + share
    local_out = w2.shape[1]
    hc, hs, wd = cols // 2, share // 2, cols // 8
    n2 = 2 * pool
    pieces = 4
    piece = local_out // pieces
    V, D = pltpu.VMEM, pltpu.SemaphoreType.DMA
    total = block_route.shape[0]
    scratch = [
        V((3, feat, width), bf16), V(w1.shape, bf16), V(w2.shape, bf16), V((4, feat, feat), bf16),
        V((5, feat, 1), f32), V((2, local_out, 1), f32), V((slots, block_len, 1), f32),
        V((pool, total * merged_rows, out_cols), bf16), D((3,)),
        V((2, 4, feat, hc), bf16), V((4, 8, row_len), f32), V((4, feat, feat), bf16),
        V((4, feat, 1), f32), V((width, hc), bf16), V((3, feat, hc), bf16),
        V((2, 4, feat, hc), bf16), V((pool, 2, 4, feat, wd), bf16), V((n2, 2, hs, wd), bf16),
        V((n2, hs, wd), bf16), V((n2, hs, wd), bf16), V((n2, hs, wd), bf16),
        V((2, hs, n2 * wd), bf16), V((pool, share, out_cols), bf16),
        V((pool, pieces, piece, out_cols), bf16), V((pool, pieces, piece, out_cols), bf16),
        V((pool, pieces, piece, out_cols), bf16),
        V((2, 4, 8, hc), f32), V((4, 8, out_cols), f32), V((piece, out_cols), f32),
        D((2, 3)), D((2, 4)), D((2, 3)), D((2, 4)), D((3,)), D((4,)), D((3,)), D((4,)),
        D((2, 3)), D((2, 4)), D((2, pool, 2)), D((pool, 2)),
        D((n2,)), D((n2,)), D((n2,)), D((n2,)), D((n2,)), D((n2,)),
        D((pool, pieces)), D((pool, pieces)), D((pool, pieces)), D((3,)), D((4,)),
    ]
    shape = jax.ShapeDtypeStruct((local_out, out_cols), bf16)
    vm = pl.BlockSpec(memory_space=pltpu.VMEM)
    return pl.pallas_call(
        functools.partial(fused_kernel, width, local_out * 4),
        out_shape=(shape, shape),
        in_specs=[vm, vm, pl.BlockSpec(memory_space=pltpu.SMEM)]
        + [vm] * 8
        + [pl.BlockSpec(memory_space=pl.ANY)] * 3,
        out_specs=(vm, vm),
        scratch_shapes=scratch,
        compiler_params=pltpu.CompilerParams(
            collective_id=0, has_side_effects=True, vmem_limit_bytes=60 << 20
        ),
        name="vision_fused",
    )(
        patches, window_ids, block_route, norm_gain, qkv_bias, proj_weight,
        proj_bias, merge_gain, b1, b2[None, :], llm_gain[None, :],
        qkv_weight.transpose(0, 2, 1), w1, w2,
    )


def fused_fits(mesh):
    return mesh.shape["tensor"] == 2 and mesh.shape["sub"] == 2 and mesh.shape["pool"] == 4


def solution(mesh):
    placed = (
        P(("tensor", "sub"), ("groups", "pool")),
        P(("groups", "pool"), None),
        P("groups"),
        P(("tensor", "sub")),
        P(None, None, ("tensor", "sub")),
        P(None, ("tensor", "sub")),
        P(("tensor", "sub"), None),
        P(("tensor", "sub")),
        P(("tensor", "sub")),
        P(None, ("tensor", "sub"), "pool"),
        P(("tensor", "sub")),
        P("pool", ("tensor", "sub")),
        P(("tensor", "sub")),
        P(("tensor", "sub")),
    )
    return jax.shard_map(
        fused_shards if fused_fits(mesh) else shards,
        mesh=mesh,
        in_specs=placed,
        out_specs=(
            P(("tensor", "sub"), ("groups", "pool")),
            P(("tensor", "sub"), ("groups", "pool")),
        ),
        check_vma=False,
    )
```
